128 devices in a mesh: tm: 16 (over x_hi, y, core), pix: 8 (over x_lo, z).
Axes of the slice: x: 4 (x_hi: 2, x_lo: 2; x = x_hi * 2 + x_lo), y: 4, z: 4, core: 2. Of those that a mesh axis runs over, the one named last changes fastest.
Arguments:
- intensity: bfloat16 [1024, 65536], P('tm', 'pix'), as said below
- labels: int32 [65536], P('pix'), may hold values from 0 to 31, as said below
Outputs:
- correlation: float32 [32, 1024, 1024], P('pix', 'tm')
The draws below stay inside these ranges and needn't reach their ends.
Inputs may be any that keep to these rules, and one draw needn't show every extreme that they name: `labels`: each aligned run of 128 pixels carries one label; within each device's block of 8192 pixels the runs go in non-decreasing label order, every q-cycle holds between 1 and 4 runs there, and some q-cycle holds exactly 4. `intensity`: every entry is positive.
All inputs are finite; a program needn't handle non-finite values.
Results may differ from the reference program's by a relative error of at most 0.0003.
Values may be sent and summed in bfloat16 or wider, within the bound.
A program may use at most 128 MiB of HBM per device.

```python
import math
import jax
import jax.numpy as jnp
from jax import lax

CYCLES = 32
PIX_DEV = 8192
CAP = 4
FRAMES = 1024
PIXELS = 65536


def draw_intensity(key, part):
    key = jax.random.fold_in(key, 11)
    keys = jax.random.split(key, 5)
    pixel_scale = jnp.exp(jax.random.uniform(keys[0], (1, PIXELS), jnp.float32, 0.0, math.log(10.0)))
    frame_scale = jnp.exp(jax.random.uniform(keys[1], (FRAMES, 1), jnp.float32, math.log(0.5), math.log(5.0)))
    rates = jnp.exp(jax.random.uniform(keys[2], (1, PIXELS), jnp.float32, math.log(0.003), math.log(0.5)))
    phases = jax.random.uniform(keys[3], (1, PIXELS), jnp.float32, -math.pi, math.pi)
    times = jnp.arange(FRAMES, dtype=jnp.float32)[:, None]
    noise = jax.random.uniform(keys[4], (FRAMES, PIXELS), jnp.float32, -0.5, 0.5)
    values = 1.5 + 0.8 * jnp.cos(rates * times + phases) + noise
    return (pixel_scale * frame_scale * values).astype(jnp.bfloat16)


def draw_labels(key, part):
    key = jax.random.fold_in(key, 5)
    blocks = PIXELS // PIX_DEV
    tiles_dev = PIX_DEV // 128
    extra_slots = (CYCLES - 1) * (CAP - 1)
    spare = tiles_dev - CYCLES - (CAP - 1)
    cycles_all = jnp.arange(CYCLES, dtype=jnp.int32)

    def one_block(block_key):
        first, second = jax.random.split(block_key, 2)
        full_cycle = jax.random.randint(first, (), 0, CYCLES, dtype=jnp.int32)
        order = jax.random.permutation(second, extra_slots).astype(jnp.int32)
        chosen = (order < spare).astype(jnp.int32)
        slot_cycle = jnp.arange(extra_slots, dtype=jnp.int32) // (CAP - 1)
        slot_cycle = slot_cycle + (slot_cycle >= full_cycle).astype(jnp.int32)
        hits = (slot_cycle[:, None] == cycles_all[None, :]).astype(jnp.int32) * chosen[:, None]
        counts = 1 + jnp.sum(hits, axis=0) + (CAP - 1) * (cycles_all == full_cycle).astype(jnp.int32)
        ends = jnp.cumsum(counts)
        place = jnp.arange(tiles_dev, dtype=jnp.int32)
        return jnp.sum((ends[None, :] <= place[:, None]).astype(jnp.int32), axis=1)
    tile_lab = jax.vmap(one_block)(jax.random.split(key, blocks))
    return jnp.repeat(tile_lab.reshape(-1), 128).astype(jnp.int32)


def setup_inputs(seed: int = 0) -> dict:
    key_list = jax.random.split(jax.random.key(seed), 3)
    intensity = draw_intensity(jax.random.fold_in(key_list[2], 71), 0)
    labels = draw_labels(jax.random.fold_in(key_list[2], 71), 0)
    return dict(intensity=intensity, labels=labels)


def reference(intensity, labels):
    num_tiles = PIXELS // 128
    picks = (PIXELS // PIX_DEV) * CAP
    tiles = intensity.reshape(FRAMES, num_tiles, 128)
    tile_lab = labels.reshape(num_tiles, 128)[:, 0]
    places = jnp.arange(num_tiles, dtype=jnp.int32)

    def one_cycle(cycle):
        keyed = jnp.where(tile_lab == cycle, places, places + num_tiles).astype(jnp.int32)
        order = jnp.argsort(keyed)[:picks].astype(jnp.int32)
        keep = tile_lab[order] == cycle
        chosen = jnp.take(tiles, order, axis=1)
        chosen = jnp.where(keep[None, :, None], chosen, jnp.zeros_like(chosen))
        flat = chosen.reshape(FRAMES, picks * 128)
        gram = jnp.dot(flat, flat.T, preferred_element_type=jnp.float32)
        totals = jnp.sum(flat, axis=1, dtype=jnp.float32)
        count = jnp.sum(keep.astype(jnp.float32)) * 128.0
        return gram * count / (totals[:, None] * totals[None, :])

    return lax.map(one_cycle, jnp.arange(CYCLES, dtype=jnp.int32))
```

```python
import jax
import jax.numpy as jnp
from jax import lax
from jax.experimental import pallas as pl
from jax.experimental.pallas import tpu as pltpu
from jax.sharding import PartitionSpec as P

CYCLES = 32
CAP = 4
MESH = pl.DeviceIdType.MESH
F32 = jnp.float32
BF16 = jnp.bfloat16
ROWS_A = 64
ROWS_B = 128
ROWS_C = 104


def nt(left, right):
    return lax.dot_general(left, right, (((1,), (1,)), ((), ())), preferred_element_type=F32)


def kernel(
    places, masks, counts, x_ref, out_ref,
    obuf, y1buf, fbuf, y2buf,
    ga, gb, gc, ra1, ra2, ra3, rb1, rb2, rb3, rc1, rc2, rc3,
    s12, s3, s4, s5, s6, r12, r3, r4, r5, r6, kept1, kept2,
    gs, gr, as_, ar, bs, br, cs, cr, fs, fr,
):
    tm, pix = lax.axis_index("tm"), lax.axis_index("pix")
    core = tm % 2
    y = (tm // 2) % 4
    kx = tm // 8
    ky = y // 2
    z = pix % 4
    xl = pix // 4
    sib = 1 - core

    def at(k, yy, c):
        return ((k * 4 + yy % 4) * 2 + c, pix)

    def flip(a, b):
        return (a + b) % 2

    z1 = z + 1 - 2 * (z % 2)
    z3 = 3 - z
    z2 = (z + 2) % 4
    dev_sib = at(kx, y, sib)
    dev_z1 = (tm, xl * 4 + z1)
    dev_z3 = (tm, xl * 4 + z3)
    dev_x = (tm, (1 - xl) * 4 + z)

    barrier = pltpu.get_barrier_semaphore()
    friends = [dev_sib, dev_z1, dev_z3, dev_x]
    for c in range(2):
        friends += [at(kx, y + 1, c), at(kx, y + 3, c), at(kx, y + 2, c), at(1 - kx, y, c)]
    for d in friends:
        pl.semaphore_signal(barrier, inc=1, device_id=d, device_id_type=MESH)
    mine = pl.ds(core * 64, 64)
    for t in range(x_ref.shape[1] // 128):
        obuf[t, mine] = x_ref[:, t * 128 : t * 128 + 128]
    pl.semaphore_wait(barrier, len(friends))

    def send(src, dst, ss, rs, k, d):
        r = pltpu.make_async_remote_copy(
            src_ref=src, dst_ref=dst, send_sem=ss.at[k], recv_sem=rs.at[k],
            device_id=d, device_id_type=MESH,
        )
        r.start()
        return r

    every = pl.ds(0, obuf.shape[0])
    src = obuf.at[every, mine]
    cp_sib = send(src, obuf.at[every, mine], gs, gr, 0, dev_sib)
    cp_f = send(src, fbuf.at[every, mine], gs, gr, 1, at(1 - kx, y, core))
    cp_y1 = send(src, y1buf.at[every, mine], gs, gr, 2, at(kx, y + 3, core))
    cp_y2 = send(src, y2buf, gs, gr, 3, at(kx, y + 2, flip(core, 1 - ky)))

    fk = pl.ds(flip(core, kx) * 64, 64)

    def span(r):
        tile = places[r]
        mask = jnp.broadcast_to(masks[pl.ds(r, 1), :], (8, CAP * 128)).astype(BF16)
        return tile, mask, counts[pl.ds(r, 1), :]

    def window(ref, tile, rows):
        return jnp.concatenate([ref[tile + k, rows] for k in range(CAP)], axis=1)

    def slot(r):
        return r // 16, (r // 4) % 4, r % 4

    def compute_a():
        @pl.loop(0, CYCLES)
        def _(r):
            tile, mask, _ = span(r)
            right = window(obuf, tile, slice(None)) * mask[0:1]
            ga[slot(r)] = nt(window(obuf, tile, mine), right)

    def compute_b():
        @pl.loop(0, CYCLES)
        def _(r):
            tile, mask, _ = span(r)
            right = jnp.concatenate([window(obuf, tile, mine), window(fbuf, tile, mine)], axis=0) * mask[0:1]
            gb[slot(r)] = nt(window(y1buf, tile, slice(None)), right)

    def compute_c():
        @pl.loop(0, CYCLES)
        def _(r):
            tile, mask, count = span(r)
            right = jnp.concatenate([window(obuf, tile, mine), window(fbuf, tile, mine)], axis=0)
            far = jnp.concatenate([window(y2buf, tile, slice(None)), window(fbuf, tile, fk)], axis=0)
            masked = right * mask[0:1]
            both = nt(far, masked)
            i, k, j = slot(r)
            gc[i, k, j, 0:64] = both[0:64]
            gc[i, k, j, 64:96] = jnp.concatenate([both[64:96, 0:64], both[96:128, 0:64]], axis=1)
            t0 = nt(mask, window(obuf, tile, slice(None)))
            t1 = nt(mask, window(y1buf, tile, slice(None)))
            t2 = nt(mask, right)
            t3 = nt(mask, far)
            row = lax.broadcasted_iota(jnp.int32, (8, 128), 0)
            stats = jnp.where(row == 0, t0, jnp.where(row == 1, t1, jnp.where(row == 2, t2, t3)))
            gc[i, k, j, 96:104] = jnp.where(row < 4, stats, count)

    lo, hi = pl.ds(0, 2), pl.ds(2, 2)
    both_x = pl.ds(0, 2)

    class Sum:
        def __init__(self, g, r1, r2, r3, ss, rs):
            self.g, self.r1, self.r2, self.r3, self.ss, self.rs = g, r1, r2, r3, ss, rs

        def first(self):
            g, r1 = self.g, self.r1
            self.c1 = [
                send(g.at[both_x, z2, lo], r1.at[0, 0], self.ss, self.rs, 0, dev_z1),
                send(g.at[both_x, z2, hi], r1.at[1, 0], self.ss, self.rs, 1, dev_z3),
                send(g.at[both_x, z1, lo], r1.at[0, 1], self.ss, self.rs, 2, dev_z1),
                send(g.at[both_x, z3, hi], r1.at[1, 1], self.ss, self.rs, 3, dev_z3),
            ]

        def second(self):
            g, r1, r2 = self.g, self.r1, self.r2
            self.c2 = []
            for p, (js, zz, d) in enumerate(((0, z3, dev_z3), (2, z1, dev_z1))):
                self.c1[p].wait()
                for i in range(2):
                    for j in range(2):
                        g[i, zz, js + j] += r1[p, 0, i, j]
                self.c2.append(send(g.at[both_x, zz, pl.ds(js, 2)], r2.at[p], self.ss, self.rs, 4 + p, d))
            for p in range(2):
                self.c1[2 + p].wait()
                for i in range(2):
                    for j in range(2):
                        g[i, z, 2 * p + j] += r1[p, 1, i, j]

        def third(self):
            g, r2 = self.g, self.r2
            for p in range(2):
                self.c2[p].wait()
                for j in range(2):
                    g[1 - xl, z, 2 * p + j] += r2[p, 1 - xl, j]
            self.c3 = send(g.at[1 - xl, z], self.r3, self.ss, self.rs, 6, dev_x)
            for p in range(2):
                for j in range(2):
                    g[xl, z, 2 * p + j] += r2[p, xl, j]

        def last(self):
            self.c3.wait()

        def total(self, j):
            return self.g[xl, z, j] + self.r3[j]

    sum_a = Sum(ga, ra1, ra2, ra3, as_, ar)
    sum_b = Sum(gb, rb1, rb2, rb3, bs, br)
    sum_c = Sum(gc, rc1, rc2, rc3, cs, cr)

    cp_sib.wait()
    compute_a()
    sum_a.first()
    cp_f.wait()
    fw_f = send(fbuf.at[every, mine], fbuf.at[every, mine], gs, gr, 4, dev_sib)
    cp_y1.wait()
    fw_y1 = send(y1buf.at[every, mine], y1buf.at[every, mine], gs, gr, 5, dev_sib)
    sum_a.second()
    fw_f.wait()
    fw_y1.wait()
    compute_b()
    sum_b.first()
    sum_a.third()
    cp_y2.wait()
    compute_c()
    sum_c.first()
    sum_b.second()
    sum_c.second()
    sum_b.third()
    sum_c.third()
    sum_a.last()
    sum_b.last()
    sum_c.last()

    here = kx * 4 + y
    near = kx * 4 + (y + 1) % 4
    prev = kx * 4 + (y + 3) % 4
    opp = kx * 4 + (y + 2) % 4
    cross = (1 - kx) * 4 + y
    cross_near = (1 - kx) * 4 + (y + 1) % 4
    cross_prev = (1 - kx) * 4 + (y + 3) % 4
    cross_opp = (1 - kx) * 4 + (y + 2) % 4
    k2 = flip(core, ky)
    k1 = flip(core, kx)

    def place(j, chip, value):
        out_ref[j, :, pl.ds(pl.multiple_of(chip * 128, 128), 128)] = value

    def ordered(k, local, remote):
        first = jnp.where(k == 0, local, remote)
        second = jnp.where(k == 0, remote, local)
        return jnp.concatenate([first, second], axis=1)

    for j in range(4):
        c_all = sum_c.total(j)
        stats = c_all[96:104]
        cols = stats.T
        count = stats[4:5]
        t_all, t_right = stats[0:1], stats[2:3]
        place(j, here, sum_a.total(j) * count / (cols[0:64, 2:3] * t_all))
        b = sum_b.total(j) * count / (cols[:, 1:2] * t_right)
        s12[0, j] = b[0:64]
        s12[1, j] = b[64:128]
        bt = b.T
        place(j, near, bt[0:64])
        s4[j] = bt[64:128]
        c2 = c_all[0:64] * count / (cols[0:64, 3:4] * t_right)
        s3[j] = c2
        c2t = c2.T
        kept2[j] = c2t[0:64]
        s5[j] = jnp.concatenate([c2t[64:96], c2t[96:128]], axis=1)
        f = jnp.concatenate([c_all[64:96, 0:64], c_all[64:96, 64:128]], axis=0)
        f = f * count[:, 0:64] / (cols[64:128, 3:4] * t_right[:, 0:64])
        s6[j] = jnp.concatenate([f[0:32], f[32:64]], axis=1)
        kept1[j] = f.T

    def copy12(k, landing):
        return pltpu.make_async_remote_copy(
            src_ref=s12.at[k], dst_ref=r12.at[landing], send_sem=fs.at[k], recv_sem=fr.at[landing],
            device_id=at(kx, y + 1, k), device_id_type=MESH,
        )

    for k in range(2):
        copy12(k, core).start()
    m = [
        send(s3, r3, fs, fr, 2, at(kx, y + 2, k2)),
        send(s4, r4, fs, fr, 3, at(1 - kx, y, core)),
        send(s5, r5, fs, fr, 4, at(1 - kx, y, core)),
        send(s6, r6, fs, fr, 5, at(1 - kx, y, k1)),
    ]
    for k in range(2):
        copy12(k, core).wait_send()
        copy12(k, k).wait_recv()
    for c in m:
        c.wait()

    for j in range(4):
        p, q = r12[0, j], r12[1, j]
        place(j, prev, jnp.concatenate([p[:, 0:64], q[:, 0:64]], axis=1))
        place(j, cross_prev, jnp.concatenate([p[:, 64:128], q[:, 64:128]], axis=1))
        place(j, cross_near, r4[j])
        far = r3[j]
        place(j, opp, ordered(k2, kept2[j], far[:, 0:64]))
        five = r5[j]
        five = jnp.concatenate([five[:, 0:64], five[:, 64:128]], axis=0)
        place(j, cross_opp, ordered(k2, five, far[:, 64:128]))
        six = r6[j]
        six = jnp.concatenate([six[:, 0:64], six[:, 64:128]], axis=0)
        place(j, cross, ordered(k1, kept1[j], six))


def per_device(intensity, labels):
    tile_lab = labels.reshape(-1, 128)[:, 0]
    cycles = jnp.arange(CYCLES, dtype=jnp.int32)
    first = jnp.sum((tile_lab[None, :] < cycles[:, None]).astype(jnp.int32), axis=1)
    count = jnp.sum((tile_lab[None, :] == cycles[:, None]).astype(jnp.int32), axis=1)
    places = jnp.minimum(first, tile_lab.shape[0] - CAP)
    low = (first - places) * 128
    high = low + count * 128
    lane = jnp.arange(CAP * 128, dtype=jnp.int32)[None, :]
    masks = ((lane >= low[:, None]) & (lane < high[:, None])).astype(F32)
    counts = jnp.broadcast_to((count * 128).astype(F32)[:, None], (CYCLES, 128))
    pix_dev = intensity.shape[1]
    dma = pltpu.SemaphoreType.DMA

    def sums(rows):
        return [
            pltpu.VMEM((2, 2, 2, 2, rows, 128), F32),
            pltpu.VMEM((2, 2, 2, rows, 128), F32),
            pltpu.VMEM((4, rows, 128), F32),
        ]

    messages = [
        pltpu.VMEM((2, 4, 64, 128), F32),
        pltpu.VMEM((4, 64, 128), F32),
        pltpu.VMEM((4, 64, 128), F32),
        pltpu.VMEM((4, 32, 128), F32),
        pltpu.VMEM((4, 32, 128), F32),
    ]
    return pl.pallas_call(
        kernel,
        out_shape=jax.ShapeDtypeStruct((4, 64, 1024), F32),
        in_specs=[
            pl.BlockSpec(memory_space=pltpu.SMEM),
            pl.BlockSpec(memory_space=pltpu.VMEM),
            pl.BlockSpec(memory_space=pltpu.VMEM),
            pl.BlockSpec(memory_space=pltpu.VMEM),
        ],
        out_specs=pl.BlockSpec(memory_space=pltpu.VMEM),
        scratch_shapes=[
            pltpu.VMEM((pix_dev // 128, 128, 128), BF16),
            pltpu.VMEM((pix_dev // 128, 128, 128), BF16),
            pltpu.VMEM((pix_dev // 128, 128, 128), BF16),
            pltpu.VMEM((pix_dev // 128, 64, 128), BF16),
            pltpu.VMEM((2, 4, 4, ROWS_A, 128), F32),
            pltpu.VMEM((2, 4, 4, ROWS_B, 128), F32),
            pltpu.VMEM((2, 4, 4, ROWS_C, 128), F32),
            *sums(ROWS_A), *sums(ROWS_B), *sums(ROWS_C),
            *messages, *messages,
            pltpu.VMEM((4, 64, 64), F32),
            pltpu.VMEM((4, 64, 64), F32),
            dma((6,)), dma((6,)), dma((7,)), dma((7,)), dma((7,)), dma((7,)),
            dma((7,)), dma((7,)), dma((6,)), dma((6,)),
        ],
        compiler_params=pltpu.CompilerParams(
            collective_id=0, has_side_effects=True, vmem_limit_bytes=48 * 2**20
        ),
    )(places, masks, counts, intensity)


def solution(mesh):
    placed = (P("tm", "pix"), P("pix"))
    return jax.shard_map(
        per_device, mesh=mesh, in_specs=placed, out_specs=P("pix", "tm", None), check_vma=False
    )
```

```python
import jax
import jax.numpy as jnp
from jax import lax
from jax.experimental import pallas as pl
from jax.experimental.pallas import tpu as pltpu
from jax.sharding import PartitionSpec as P

CYCLES = 32
CAP = 4
MESH = pl.DeviceIdType.MESH
F32 = jnp.float32
BF16 = jnp.bfloat16
FRAMES_DEV = 64
TOP = 32768.0
STEPS = 2048.0
CODE = jnp.int16
SUMS = (64, 64, 96, 64)
RELAYED = 44


def nt(left, right):
    return lax.dot_general(left, right, (((1,), (1,)), ((), ())), preferred_element_type=F32)


def encode(value):
    level = jnp.log2(jnp.maximum(value, 1.0 / 65536.0)) * STEPS
    return jnp.round(level).astype(jnp.int32).astype(CODE)


def decode(code):
    return jnp.exp2(code.astype(jnp.int32).astype(F32) * (1.0 / STEPS))


def fold(block):
    return jnp.concatenate([block[0:32], block[32:64]], axis=1)


def unfold(block):
    return jnp.concatenate([block[:, 0:64], block[:, 64:128]], axis=0)


def kernel(places, masks, counts, x_ref, out_ref, *refs):
    refs = list(refs)

    def take(n):
        got = refs[:n]
        del refs[:n]
        return got

    xv, ownb, obuf, fbuf, y1buf, y2buf, relay = take(7)
    part, landed, tt, tr = take(4)
    col_y1, col_y2, col_f = take(3)
    row_o, row_f, row_2 = take(3)
    sets = [take(9) for _ in SUMS]
    s1, s2, s3, s4, s5, s6, s7 = take(7)
    r1, r2, r3, r4, r5, r6, r7 = take(7)
    kept0, kept1, kept2 = take(3)
    own_sem, gs, gr, ps, pr, ts, tsr, fs, fr = take(9)

    tm, pix = lax.axis_index("tm"), lax.axis_index("pix")
    core = tm % 2
    y = (tm // 2) % 4
    kx = tm // 8
    ky = y // 2
    z = pix % 4
    xl = pix // 4
    sib = 1 - core

    def at(k, yy, c):
        return ((k * 4 + yy % 4) * 2 + c, pix)

    def flip(a, b):
        return (a + b) % 2

    k2 = flip(core, ky)
    k1 = flip(core, kx)
    z1 = z + 1 - 2 * (z % 2)
    z3 = 3 - z
    z2 = (z + 2) % 4
    dev_sib = at(kx, y, sib)
    dev_z1 = (tm, xl * 4 + z1)
    dev_z3 = (tm, xl * 4 + z3)
    dev_x = (tm, (1 - xl) * 4 + z)
    near_core = at(kx, y + 1, core)

    own = pltpu.make_async_copy(x_ref, xv, own_sem)
    own.start()
    barrier = pltpu.get_barrier_semaphore()
    friends = [dev_sib] + [(tm, (pix + q) % 8) for q in range(1, 8)]
    for c in range(2):
        friends += [at(kx, y + 1, c), at(kx, y + 3, c), at(kx, y + 2, c), at(1 - kx, y, c)]
    for d in friends:
        pl.semaphore_signal(barrier, inc=1, device_id=d, device_id_type=MESH)
    mine = pl.ds(core * 64, 64)
    own.wait()
    for t in range(x_ref.shape[1] // 128):
        block = xv[:, t * 128 : t * 128 + 128]
        ownb[t] = block
        obuf[t, mine] = block
    pl.semaphore_wait(barrier, len(friends))

    def copy(src, dst, ss, rs, d):
        return pltpu.make_async_remote_copy(
            src_ref=src, dst_ref=dst, send_sem=ss, recv_sem=rs, device_id=d, device_id_type=MESH
        )

    def send(src, dst, ss, rs, k, d):
        r = copy(src, dst, ss.at[k], rs.at[k], d)
        r.start()
        return r

    every = pl.ds(0, obuf.shape[0])
    pre = pl.ds(0, RELAYED)
    post = pl.ds(RELAYED, obuf.shape[0] - RELAYED)
    dev_prev = at(kx, y + 3, core)
    cp_y1p = send(ownb.at[post], y1buf.at[post], gs, gr, 1, dev_prev)
    cp_rel = send(ownb.at[pre], relay, gs, gr, 2, near_core)
    cp_y1q = send(ownb.at[pre], y1buf.at[pre], gs, gr, 5, dev_prev)
    cp_sib = send(ownb, obuf.at[every, mine], gs, gr, 0, dev_sib)

    def span(r):
        tile = places[r]
        mask = jnp.broadcast_to(masks[pl.ds(r, 1), :], (8, CAP * 128)).astype(BF16)
        return tile, mask

    def window(ref, tile, rows):
        return jnp.concatenate([ref[tile + k, rows] for k in range(CAP)], axis=1)

    def slot(r):
        return r // 16, (r // 4) % 4, r % 4

    def cycles(body):
        @pl.loop(0, CYCLES, unroll=4)
        def _(r):
            body(r)

    ga, gb, gd, gc = [q[0] for q in sets]
    whole = slice(None)

    def scaled(r, g, col, rows):
        return g * col * rows[pl.ds(r, 1), :]

    def totals_own(r):
        tile, mask = span(r)
        t = nt(mask, window(ownb, tile, whole))
        part[pl.ds(r, 1)] = jnp.concatenate([t[0:1], counts[pl.ds(r, 1), 0:64]], axis=1)

    def gram_a(r):
        tile, mask = span(r)
        right = window(obuf, tile, whole) * mask[0:1]
        ga[slot(r)] = nt(window(obuf, tile, mine), right)

    def gram_b(r):
        tile, mask = span(r)
        right = window(obuf, tile, whole) * mask[0:1]
        gb[slot(r)] = scaled(r, nt(window(y1buf, tile, whole), right), col_y1[r], row_o)

    def two(tile, mask):
        right = jnp.concatenate([window(obuf, tile, mine), window(fbuf, tile, mine)], axis=0)
        return right * mask[0:1]

    def gram_d(r):
        tile, mask = span(r)
        i, k, j = slot(r)
        right = window(fbuf, tile, whole) * mask[0:1]
        gd[i, k, j, 0:64] = scaled(r, nt(window(y1buf, tile, whole), right), col_y1[r], row_f)
        fk = pl.ds(k1 * 64, 64)
        right = window(obuf, tile, mine) * mask[0:1]
        g = nt(window(fbuf, tile, fk), right)
        g = g * col_f[r, :, 0:64] * row_2[pl.ds(r, 1), 0:64]
        gd[i, k, j, 64:96] = fold(g)

    def gram_c(r):
        tile, mask = span(r)
        g = nt(window(y2buf, tile, whole), two(tile, mask))
        gc[slot(r)] = scaled(r, g, col_y2[r], row_2)

    lo, hi = pl.ds(0, 2), pl.ds(2, 2)
    both_x = pl.ds(0, 2)

    class Sum:
        def __init__(self, coded, g, e1, e2, e3, r1, r2, r3, ss, rs):
            self.encode = encode if coded else (lambda v: v)
            self.decode = decode if coded else (lambda v: v)
            self.g, self.e, self.r = g, (e1, e2, e3), (r1, r2, r3)
            self.ss, self.rs = ss, rs

        def first(self):
            g, e1, r1 = self.g, self.e[0], self.r[0]
            self.c1 = []
            for w, (za, zb) in enumerate(((z2, z2), (z1, z3))):
                for p, (js, zz, d) in enumerate(((0, za, dev_z1), (2, zb, dev_z3))):
                    for i in range(2):
                        for j in range(2):
                            e1[p, w, i, j] = self.encode(g[i, zz, js + j])
                    self.c1.append(send(e1.at[p, w], r1.at[p, w], self.ss, self.rs, 2 * w + p, d))

        def second(self):
            g, e2, r1, r2 = self.g, self.e[1], self.r[0], self.r[1]
            self.c2 = []
            for p, (js, zz, d) in enumerate(((0, z3, dev_z3), (2, z1, dev_z1))):
                self.c1[p].wait()
                for i in range(2):
                    for j in range(2):
                        e2[p, i, j] = self.encode(g[i, zz, js + j] + self.decode(r1[p, 0, i, j]))
                self.c2.append(send(e2.at[p], r2.at[p], self.ss, self.rs, 4 + p, d))
            for p in range(2):
                self.c1[2 + p].wait()
                for i in range(2):
                    for j in range(2):
                        g[i, z, 2 * p + j] += self.decode(r1[p, 1, i, j])

        def third(self):
            g, e3, r2 = self.g, self.e[2], self.r[1]
            for p in range(2):
                self.c2[p].wait()
                for j in range(2):
                    e3[2 * p + j] = self.encode(g[1 - xl, z, 2 * p + j] + self.decode(r2[p, 1 - xl, j]))
            self.c3 = send(e3, self.r[2], self.ss, self.rs, 6, dev_x)
            for p in range(2):
                for j in range(2):
                    g[xl, z, 2 * p + j] += self.decode(r2[p, xl, j])

        def last(self):
            self.c3.wait()

        def total(self, j):
            return self.g[xl, z, j] + self.decode(self.r[2][j])

    sum_a, sum_b, sum_d, sum_c = [Sum(n > 0, *q) for n, q in enumerate(sets)]

    cycles(totals_own)
    cp = []
    for q in range(1, 8):
        cp.append(send(part, landed.at[q - 1], ps, pr, q - 1, (tm, (pix + q) % 8)))
    cp_f = send(ownb, fbuf.at[every, mine], gs, gr, 3, at(1 - kx, y, core))
    cp_sib.wait()
    cycles(gram_a)
    sum_a.first()
    cp_y1p.wait()
    cp_fp = send(y1buf.at[post], y2buf.at[post], gs, gr, 6, at(kx, y + 3, flip(core, ((y + 3) % 4) // 2)))
    total = part[...]
    for q in range(7):
        cp[q].wait()
        total = total + landed[q]
    tt[...] = total
    tcopies = [
        send(tt, tr.at[0], ts, tsr, 0, dev_sib),
        send(tt, tr.at[1], ts, tsr, 1, dev_prev),
        send(tt, tr.at[2], ts, tsr, 2, at(kx, y + 2, flip(core, 1 - ky))),
    ]

    def tcopy(to, slot_core):
        return copy(tt, tr.at[3 + slot_core], ts.at[3 + to], tsr.at[3 + slot_core], at(1 - kx, y, to))

    for c in range(2):
        tcopy(c, core).start()
    sum_a.second()
    cp_rel.wait()
    cp_fr = send(relay, y2buf.at[pre], gs, gr, 7, at(kx, y + 1, flip(core, ((y + 1) % 4) // 2)))
    sum_a.third()
    for c in tcopies:
        c.wait()
    for c in range(2):
        tcopy(c, core).wait_send()
        tcopy(c, c).wait_recv()

    def pair(first, second):
        return 1.0 / jnp.concatenate([first[:, 0:64], second[:, 0:64]], axis=1)

    def fill(col, table):
        up = (TOP / table.T)[0:64]
        for r in range(CYCLES):
            col[r] = jnp.broadcast_to(up[:, r : r + 1], (64, 128))

    mine_t, sib_t, f0_t, f1_t = tt[...], tr[0], tr[3], tr[4]
    row_o[...] = jnp.where(core == 0, pair(mine_t, sib_t), pair(sib_t, mine_t))
    row_f[...] = pair(f0_t, f1_t)
    row_2[...] = pair(mine_t, jnp.where(core == 0, f0_t, f1_t))
    fill(col_y1, tr[1])

    here = kx * 4 + y
    near = kx * 4 + (y + 1) % 4
    prev = kx * 4 + (y + 3) % 4
    opp = kx * 4 + (y + 2) % 4
    cross = (1 - kx) * 4 + y
    cross_near = (1 - kx) * 4 + (y + 1) % 4
    cross_prev = (1 - kx) * 4 + (y + 3) % 4
    cross_opp = (1 - kx) * 4 + (y + 2) % 4

    def place(j, chip, value):
        value = value * (count(j) * (1.0 / TOP))
        out_ref[j, :, pl.ds(pl.multiple_of(chip * 128, 128), 128)] = value

    def ordered(k, local, remote):
        first = jnp.where(k == 0, local, remote)
        second = jnp.where(k == 0, remote, local)
        return jnp.concatenate([first, second], axis=1)

    def count(j):
        return tt[pl.ds(pix * 4 + j, 1), 64:65]

    def final_a():
        for j in range(4):
            lanes = row_o[pl.ds(pix * 4 + j, 1), :]
            up = (TOP / jnp.broadcast_to(tt[pl.ds(pix * 4 + j, 1), :], (8, 128)).T)[0:64, 0:1]
            place(j, here, sum_a.total(j) * up * lanes)

    def final_b():
        for j in range(4):
            b = sum_b.total(j)
            s1[j] = encode(b)
            bt = b.T
            kept0[j] = jnp.where(core == 0, bt[0:64], bt[64:128])
            s7[j] = encode(fold(jnp.where(core == 0, bt[64:128], bt[0:64])))
        return [
            send(s1, r1, fs, fr, 0, near_core),
            send(s7, r7, fs, fr, 1, dev_sib),
        ]

    def copy4(to, landing):
        return copy(s4.at[to], r4.at[landing], fs.at[2 + to], fr.at[2 + landing], at(1 - kx, y, to))

    def final_d():
        for j in range(4):
            g = sum_d.total(j)
            s2[j] = encode(g[0:64])
            dt = g[0:64].T
            s4[0, j] = encode(fold(dt[0:64]))
            s4[1, j] = encode(fold(dt[64:128]))
            s6[j] = encode(g[64:96])
            kept1[j] = unfold(g[64:96]).T
        for c in range(2):
            copy4(c, core).start()
        return [
            send(s2, r2, fs, fr, 4, near_core),
            send(s6, r6, fs, fr, 5, at(1 - kx, y, k1)),
        ]

    def final_c():
        for j in range(4):
            e = sum_c.total(j)
            s3[j] = encode(e)
            et = e.T
            kept2[j] = et[0:64]
            s5[j] = encode(fold(et[64:128]))
        return [
            send(s3, r3, fs, fr, 6, at(kx, y + 2, k2)),
            send(s5, r5, fs, fr, 7, at(1 - kx, y, core)),
        ]

    cp_f.wait()
    fw_f = send(fbuf.at[every, mine], fbuf.at[every, mine], gs, gr, 4, dev_sib)
    cp_y1q.wait()
    cycles(gram_b)
    sum_b.first()
    fill(col_f, jnp.where(k1 == 0, f0_t, f1_t))
    fw_f.wait()
    cycles(gram_d)
    sum_d.first()
    sum_a.last()
    final_a()
    fill(col_y2, tr[2])
    sum_b.second()
    cp_fp.wait()
    cp_fr.wait()
    cycles(gram_c)
    sum_c.first()
    sum_b.third()
    sum_d.second()
    sum_b.last()
    out_b = final_b()
    sum_d.third()
    sum_c.second()
    sum_d.last()
    out_d = final_d()
    sum_c.third()
    for c in out_b:
        c.wait()
    for j in range(4):
        place(j, near, ordered(core, kept0[j], unfold(decode(r7[j]))))
        place(j, prev, decode(r1[j]))
    sum_c.last()
    out_c = final_c()

    for c in range(2):
        copy4(c, core).wait_send()
        copy4(c, c).wait_recv()
    for c in out_d:
        c.wait()
    for j in range(4):
        place(j, cross_near, jnp.concatenate([unfold(decode(r4[0, j])), unfold(decode(r4[1, j]))], axis=1))
        place(j, cross_prev, decode(r2[j]))
        place(j, cross, ordered(k1, kept1[j], unfold(decode(r6[j]))))
    for c in out_c:
        c.wait()
    for j in range(4):
        far = decode(r3[j])
        place(j, opp, ordered(k2, kept2[j], far[:, 0:64]))
        place(j, cross_opp, ordered(k2, unfold(decode(r5[j])), far[:, 64:128]))


def per_device(intensity, labels):
    tile_lab = labels.reshape(-1, 128)[:, 0]
    cycles = jnp.arange(CYCLES, dtype=jnp.int32)
    first = jnp.sum((tile_lab[None, :] < cycles[:, None]).astype(jnp.int32), axis=1)
    count = jnp.sum((tile_lab[None, :] == cycles[:, None]).astype(jnp.int32), axis=1)
    places = jnp.minimum(first, tile_lab.shape[0] - CAP)
    low = (first - places) * 128
    high = low + count * 128
    lane = jnp.arange(CAP * 128, dtype=jnp.int32)[None, :]
    masks = ((lane >= low[:, None]) & (lane < high[:, None])).astype(F32)
    counts = jnp.broadcast_to((count * 128).astype(F32)[:, None], (CYCLES, 128))
    pix_dev = intensity.shape[1]
    dma = pltpu.SemaphoreType.DMA

    def sums(rows, code):
        halves = [
            pltpu.VMEM((2, 2, 2, 2, rows, 128), code),
            pltpu.VMEM((2, 2, 2, rows, 128), code),
            pltpu.VMEM((4, rows, 128), code),
        ]
        return [
            pltpu.VMEM((2, 4, 4, rows, 128), F32),
            *halves,
            *halves,
            dma((7,)),
            dma((7,)),
        ]

    big = pltpu.VMEM((4, 64, 128), CODE)
    small = pltpu.VMEM((4, 32, 128), CODE)
    messages = [big, big, big, pltpu.VMEM((2, 4, 32, 128), CODE), small, small, small]
    kept = pltpu.VMEM((4, 64, 64), F32)
    tiles = pix_dev // 128
    return pl.pallas_call(
        kernel,
        out_shape=jax.ShapeDtypeStruct((4, 64, 1024), F32),
        in_specs=[
            pl.BlockSpec(memory_space=pltpu.SMEM),
            pl.BlockSpec(memory_space=pltpu.VMEM),
            pl.BlockSpec(memory_space=pltpu.VMEM),
            pl.BlockSpec(memory_space=pltpu.HBM),
        ],
        out_specs=pl.BlockSpec(memory_space=pltpu.VMEM),
        scratch_shapes=[
            pltpu.VMEM((FRAMES_DEV, pix_dev), BF16),
            pltpu.VMEM((tiles, FRAMES_DEV, 128), BF16),
            pltpu.VMEM((tiles, 2 * FRAMES_DEV, 128), BF16),
            pltpu.VMEM((tiles, 2 * FRAMES_DEV, 128), BF16),
            pltpu.VMEM((tiles, FRAMES_DEV, 128), BF16),
            pltpu.VMEM((tiles, FRAMES_DEV, 128), BF16),
            pltpu.VMEM((RELAYED, FRAMES_DEV, 128), BF16),
            pltpu.VMEM((CYCLES, 128), F32),
            pltpu.VMEM((7, CYCLES, 128), F32),
            pltpu.VMEM((CYCLES, 128), F32),
            pltpu.VMEM((5, CYCLES, 128), F32),
            *[pltpu.VMEM((CYCLES, FRAMES_DEV, 128), F32)] * 3,
            *[pltpu.VMEM((CYCLES, 128), F32)] * 3,
            *[ref for n, rows in enumerate(SUMS) for ref in sums(rows, CODE if n else F32)],
            *messages,
            *messages,
            kept,
            kept,
            kept,
            dma,
            dma((8,)),
            dma((8,)),
            dma((7,)),
            dma((7,)),
            dma((5,)),
            dma((5,)),
            dma((8,)),
            dma((8,)),
        ],
        compiler_params=pltpu.CompilerParams(
            collective_id=0, has_side_effects=True, vmem_limit_bytes=48 * 2**20
        ),
    )(places, masks, counts, intensity)


def solution(mesh):
    placed = (P("tm", "pix"), P("pix"))
    return jax.shard_map(
        per_device, mesh=mesh, in_specs=placed, out_specs=P("pix", "tm", None), check_vma=False
    )
```

```python
import jax
import jax.numpy as jnp
from jax import lax
from jax.experimental import pallas as pl
from jax.experimental.pallas import tpu as pltpu
from jax.sharding import PartitionSpec as P

CYCLES = 32
CAP = 4
MESH = pl.DeviceIdType.MESH
F32 = jnp.float32
BF16 = jnp.bfloat16
FRAMES_DEV = 64
TOP = 32768.0
STEPS = 2048.0
CODE = jnp.int16
ROWS_A = 64
DIRECT = (64, 96, 64)
RELAYED = 44


def nt(left, right):
    return lax.dot_general(left, right, (((1,), (1,)), ((), ())), preferred_element_type=F32)


def encode(value):
    level = jnp.log2(jnp.maximum(value, 1.0 / 65536.0)) * STEPS
    return jnp.round(level).astype(jnp.int32).astype(CODE)


def decode(code):
    return jnp.exp2(code.astype(jnp.int32).astype(F32) * (1.0 / STEPS))


def fold(block):
    return jnp.concatenate([block[0:32], block[32:64]], axis=1)


def unfold(block):
    return jnp.concatenate([block[:, 0:64], block[:, 64:128]], axis=0)


def kernel(places, masks, counts, x_ref, out_ref, *refs):
    refs = list(refs)

    def take(n):
        got = refs[:n]
        del refs[:n]
        return got

    xv, ownb, obuf, fbuf, y1buf, y2buf, relay = take(7)
    part, landed, tt, tr = take(4)
    col_y1, col_y2, col_f = take(3)
    row_o, row_f, row_2 = take(3)
    set_a = take(9)
    sets = [take(5) for _ in DIRECT]
    s1, s2, s3, s4, s5, s6, s7 = take(7)
    r1, r2, r3, r4, r5, r6, r7 = take(7)
    kept0, kept1, kept2 = take(3)
    own_sem, gs, gr, ps, pr, ts, tsr, fs, fr = take(9)

    tm, pix = lax.axis_index("tm"), lax.axis_index("pix")
    core = tm % 2
    y = (tm // 2) % 4
    kx = tm // 8
    ky = y // 2
    z = pix % 4
    xl = pix // 4
    sib = 1 - core

    def at(k, yy, c):
        return ((k * 4 + yy % 4) * 2 + c, pix)

    def flip(a, b):
        return (a + b) % 2

    k2 = flip(core, ky)
    k1 = flip(core, kx)
    z1 = z + 1 - 2 * (z % 2)
    z3 = 3 - z
    z2 = (z + 2) % 4
    dev_sib = at(kx, y, sib)
    dev_z1 = (tm, xl * 4 + z1)
    dev_z3 = (tm, xl * 4 + z3)
    dev_x = (tm, (1 - xl) * 4 + z)
    near_core = at(kx, y + 1, core)

    own = pltpu.make_async_copy(x_ref, xv, own_sem)
    own.start()
    barrier = pltpu.get_barrier_semaphore()
    friends = [dev_sib] + [(tm, (pix + q) % 8) for q in range(1, 8)]
    for c in range(2):
        friends += [at(kx, y + 1, c), at(kx, y + 3, c), at(kx, y + 2, c), at(1 - kx, y, c)]
    for d in friends:
        pl.semaphore_signal(barrier, inc=1, device_id=d, device_id_type=MESH)
    mine = pl.ds(core * 64, 64)
    own.wait()
    for t in range(x_ref.shape[1] // 128):
        block = xv[:, t * 128 : t * 128 + 128]
        ownb[t] = block
        obuf[t, mine] = block
    pl.semaphore_wait(barrier, len(friends))

    def copy(src, dst, ss, rs, d):
        return pltpu.make_async_remote_copy(
            src_ref=src, dst_ref=dst, send_sem=ss, recv_sem=rs, device_id=d, device_id_type=MESH
        )

    def send(src, dst, ss, rs, k, d):
        r = copy(src, dst, ss.at[k], rs.at[k], d)
        r.start()
        return r

    every = pl.ds(0, obuf.shape[0])
    pre = pl.ds(0, RELAYED)
    post = pl.ds(RELAYED, obuf.shape[0] - RELAYED)
    dev_prev = at(kx, y + 3, core)
    cp_y1 = send(ownb, y1buf, gs, gr, 1, dev_prev)
    cp_rel = send(ownb.at[pre], relay, gs, gr, 2, near_core)
    cp_sib = send(ownb, obuf.at[every, mine], gs, gr, 0, dev_sib)

    def span(r):
        tile = places[r]
        mask = jnp.broadcast_to(masks[pl.ds(r, 1), :], (8, CAP * 128)).astype(BF16)
        return tile, mask

    def window(ref, tile, rows):
        return jnp.concatenate([ref[tile + k, rows] for k in range(CAP)], axis=1)

    def slot(r):
        return r // 16, (r // 4) % 4, r % 4

    def cycles(body):
        @pl.loop(0, CYCLES, unroll=4)
        def _(r):
            body(r)

    ga = set_a[0]
    whole = slice(None)

    def scaled(r, g, col, rows):
        return g * col * rows[pl.ds(r, 1), :]

    def totals_own(r):
        tile, mask = span(r)
        t = nt(mask, window(ownb, tile, whole))
        part[pl.ds(r, 1)] = jnp.concatenate([t[0:1], counts[pl.ds(r, 1), 0:64]], axis=1)

    def gram_a(r):
        tile, mask = span(r)
        right = window(obuf, tile, whole) * mask[0:1]
        ga[slot(r)] = nt(window(obuf, tile, mine), right)

    def gram_b(r):
        tile, mask = span(r)
        right = window(obuf, tile, whole) * mask[0:1]
        return scaled(r, nt(window(y1buf, tile, whole), right), col_y1[r], row_o)

    def two(tile, mask):
        right = jnp.concatenate([window(obuf, tile, mine), window(fbuf, tile, mine)], axis=0)
        return right * mask[0:1]

    def gram_d(r):
        tile, mask = span(r)
        right = window(fbuf, tile, whole) * mask[0:1]
        first = scaled(r, nt(window(y1buf, tile, whole), right), col_y1[r], row_f)
        fk = pl.ds(k1 * 64, 64)
        right = window(obuf, tile, mine) * mask[0:1]
        g = nt(window(fbuf, tile, fk), right)
        g = g * col_f[r, :, 0:64] * row_2[pl.ds(r, 1), 0:64]
        return jnp.concatenate([first, fold(g)], axis=0)

    def gram_c(r):
        tile, mask = span(r)
        g = nt(window(y2buf, tile, whole), two(tile, mask))
        return scaled(r, g, col_y2[r], row_2)

    lo, hi = pl.ds(0, 2), pl.ds(2, 2)
    both_x = pl.ds(0, 2)

    class Sum:
        def __init__(self, g, e1, e2, e3, r1, r2, r3, ss, rs):
            self.g, self.e, self.r = g, (e1, e2, e3), (r1, r2, r3)
            self.ss, self.rs = ss, rs

        def first(self):
            g, r1 = self.g, self.r[0]
            self.c1 = [
                send(g.at[both_x, z2, lo], r1.at[0, 0], self.ss, self.rs, 0, dev_z1),
                send(g.at[both_x, z2, hi], r1.at[1, 0], self.ss, self.rs, 1, dev_z3),
                send(g.at[both_x, z1, lo], r1.at[0, 1], self.ss, self.rs, 2, dev_z1),
                send(g.at[both_x, z3, hi], r1.at[1, 1], self.ss, self.rs, 3, dev_z3),
            ]

        def second(self):
            g, r1, r2 = self.g, self.r[0], self.r[1]
            self.c2 = []
            for p, (js, zz, d) in enumerate(((0, z3, dev_z3), (2, z1, dev_z1))):
                self.c1[p].wait()
                for i in range(2):
                    for j in range(2):
                        g[i, zz, js + j] += r1[p, 0, i, j]
                self.c2.append(send(g.at[both_x, zz, pl.ds(js, 2)], r2.at[p], self.ss, self.rs, 4 + p, d))
            for p in range(2):
                self.c1[2 + p].wait()
                for i in range(2):
                    for j in range(2):
                        g[i, z, 2 * p + j] += r1[p, 1, i, j]

        def third(self):
            g, r2 = self.g, self.r[1]
            for p in range(2):
                self.c2[p].wait()
                for j in range(2):
                    g[1 - xl, z, 2 * p + j] += r2[p, 1 - xl, j]
            self.c3 = send(g.at[1 - xl, z], self.r[2], self.ss, self.rs, 6, dev_x)
            for p in range(2):
                for j in range(2):
                    g[xl, z, 2 * p + j] += r2[p, xl, j]

        def last(self):
            self.c3.wait()

        def total(self, j):
            return self.g[xl, z, j] + self.r[2][j]

    class Direct:
        def __init__(self, body, own, e, r, ss, rs):
            self.body, self.own, self.e, self.r, self.ss, self.rs = body, own, e, r, ss, rs

        def copy(self, q):
            k = q - 1
            return copy(self.e.at[k], self.r.at[k], self.ss.at[k], self.rs.at[k], (tm, (pix + q) % 8))

        def run(self):
            @pl.loop(1, 8)
            def _(q):
                p = (pix + q) % 8
                for j in range(4):
                    self.e[q - 1, j] = encode(self.body(p * 4 + j))
                self.copy(q).start()

            for j in range(4):
                self.own[j] = self.body(pix * 4 + j)

        def wait(self):
            for q in range(1, 8):
                self.copy(q).wait()

        def total(self, j):
            value = self.own[j]
            for q in range(7):
                value = value + decode(self.r[q, j])
            return value

    sum_a = Sum(*set_a)
    sum_b, sum_d, sum_c = [Direct(body, *q) for body, q in zip((gram_b, gram_d, gram_c), sets)]

    cycles(totals_own)
    cp = []
    for q in range(1, 8):
        cp.append(send(part, landed.at[q - 1], ps, pr, q - 1, (tm, (pix + q) % 8)))
    cp_f = send(ownb, fbuf.at[every, mine], gs, gr, 3, at(1 - kx, y, core))
    cp_sib.wait()
    cycles(gram_a)
    sum_a.first()
    total = part[...]
    for q in range(7):
        cp[q].wait()
        total = total + landed[q]
    tt[...] = total
    tcopies = [
        send(tt, tr.at[0], ts, tsr, 0, dev_sib),
        send(tt, tr.at[1], ts, tsr, 1, dev_prev),
        send(tt, tr.at[2], ts, tsr, 2, at(kx, y + 2, flip(core, 1 - ky))),
    ]

    def tcopy(to, slot_core):
        return copy(tt, tr.at[3 + slot_core], ts.at[3 + to], tsr.at[3 + slot_core], at(1 - kx, y, to))

    for c in range(2):
        tcopy(c, core).start()
    sum_a.second()
    cp_rel.wait()
    cp_fr = send(relay, y2buf.at[pre], gs, gr, 7, at(kx, y + 1, flip(core, ((y + 1) % 4) // 2)))
    sum_a.third()
    cp_y1.wait()
    cp_fp = send(y1buf.at[post], y2buf.at[post], gs, gr, 6, at(kx, y + 3, flip(core, ((y + 3) % 4) // 2)))
    for c in tcopies:
        c.wait()
    for c in range(2):
        tcopy(c, core).wait_send()
        tcopy(c, c).wait_recv()

    def pair(first, second):
        return 1.0 / jnp.concatenate([first[:, 0:64], second[:, 0:64]], axis=1)

    def fill(col, table):
        up = (TOP / table.T)[0:64]
        for r in range(CYCLES):
            col[r] = jnp.broadcast_to(up[:, r : r + 1], (64, 128))

    mine_t, sib_t, f0_t, f1_t = tt[...], tr[0], tr[3], tr[4]
    row_o[...] = jnp.where(core == 0, pair(mine_t, sib_t), pair(sib_t, mine_t))
    row_f[...] = pair(f0_t, f1_t)
    row_2[...] = pair(mine_t, jnp.where(core == 0, f0_t, f1_t))
    fill(col_y1, tr[1])

    here = kx * 4 + y
    near = kx * 4 + (y + 1) % 4
    prev = kx * 4 + (y + 3) % 4
    opp = kx * 4 + (y + 2) % 4
    cross = (1 - kx) * 4 + y
    cross_near = (1 - kx) * 4 + (y + 1) % 4
    cross_prev = (1 - kx) * 4 + (y + 3) % 4
    cross_opp = (1 - kx) * 4 + (y + 2) % 4

    def place(j, chip, value):
        value = value * (count(j) * (1.0 / TOP))
        out_ref[j, :, pl.ds(pl.multiple_of(chip * 128, 128), 128)] = value

    def ordered(k, local, remote):
        first = jnp.where(k == 0, local, remote)
        second = jnp.where(k == 0, remote, local)
        return jnp.concatenate([first, second], axis=1)

    def count(j):
        return tt[pl.ds(pix * 4 + j, 1), 64:65]

    def final_a():
        for j in range(4):
            lanes = row_o[pl.ds(pix * 4 + j, 1), :]
            up = (TOP / jnp.broadcast_to(tt[pl.ds(pix * 4 + j, 1), :], (8, 128)).T)[0:64, 0:1]
            place(j, here, sum_a.total(j) * up * lanes)

    def final_b():
        for j in range(4):
            b = sum_b.total(j)
            s1[j] = encode(b)
            bt = b.T
            kept0[j] = jnp.where(core == 0, bt[0:64], bt[64:128])
            s7[j] = encode(fold(jnp.where(core == 0, bt[64:128], bt[0:64])))
        return [
            send(s1, r1, fs, fr, 0, near_core),
            send(s7, r7, fs, fr, 1, dev_sib),
        ]

    def copy4(to, landing):
        return copy(s4.at[to], r4.at[landing], fs.at[2 + to], fr.at[2 + landing], at(1 - kx, y, to))

    def final_d():
        for j in range(4):
            g = sum_d.total(j)
            s2[j] = encode(g[0:64])
            dt = g[0:64].T
            s4[0, j] = encode(fold(dt[0:64]))
            s4[1, j] = encode(fold(dt[64:128]))
            s6[j] = encode(g[64:96])
            kept1[j] = unfold(g[64:96]).T
        for c in range(2):
            copy4(c, core).start()
        return [
            send(s2, r2, fs, fr, 4, near_core),
            send(s6, r6, fs, fr, 5, at(1 - kx, y, k1)),
        ]

    def final_c():
        for j in range(4):
            e = sum_c.total(j)
            s3[j] = encode(e)
            et = e.T
            kept2[j] = et[0:64]
            s5[j] = encode(fold(et[64:128]))
        return [
            send(s3, r3, fs, fr, 6, at(kx, y + 2, k2)),
            send(s5, r5, fs, fr, 7, at(1 - kx, y, core)),
        ]

    cp_f.wait()
    fw_f = send(fbuf.at[every, mine], fbuf.at[every, mine], gs, gr, 4, dev_sib)
    sum_b.run()
    fill(col_f, jnp.where(k1 == 0, f0_t, f1_t))
    fw_f.wait()
    sum_d.run()
    fill(col_y2, tr[2])
    cp_fp.wait()
    cp_fr.wait()
    sum_c.run()
    sum_a.last()
    final_a()
    sum_b.wait()
    out_b = final_b()
    sum_d.wait()
    out_d = final_d()
    sum_c.wait()
    out_c = final_c()
    for c in out_b:
        c.wait()
    for j in range(4):
        place(j, near, ordered(core, kept0[j], unfold(decode(r7[j]))))
        place(j, prev, decode(r1[j]))

    for c in range(2):
        copy4(c, core).wait_send()
        copy4(c, c).wait_recv()
    for c in out_d:
        c.wait()
    for j in range(4):
        place(j, cross_near, jnp.concatenate([unfold(decode(r4[0, j])), unfold(decode(r4[1, j]))], axis=1))
        place(j, cross_prev, decode(r2[j]))
        place(j, cross, ordered(k1, kept1[j], unfold(decode(r6[j]))))
    for c in out_c:
        c.wait()
    for j in range(4):
        far = decode(r3[j])
        place(j, opp, ordered(k2, kept2[j], far[:, 0:64]))
        place(j, cross_opp, ordered(k2, unfold(decode(r5[j])), far[:, 64:128]))


def per_device(intensity, labels):
    tile_lab = labels.reshape(-1, 128)[:, 0]
    cycles = jnp.arange(CYCLES, dtype=jnp.int32)
    first = jnp.sum((tile_lab[None, :] < cycles[:, None]).astype(jnp.int32), axis=1)
    count = jnp.sum((tile_lab[None, :] == cycles[:, None]).astype(jnp.int32), axis=1)
    places = jnp.minimum(first, tile_lab.shape[0] - CAP)
    low = (first - places) * 128
    high = low + count * 128
    lane = jnp.arange(CAP * 128, dtype=jnp.int32)[None, :]
    masks = ((lane >= low[:, None]) & (lane < high[:, None])).astype(F32)
    counts = jnp.broadcast_to((count * 128).astype(F32)[:, None], (CYCLES, 128))
    pix_dev = intensity.shape[1]
    dma = pltpu.SemaphoreType.DMA

    halves = [
        pltpu.VMEM((2, 2, 2, 2, ROWS_A, 128), F32),
        pltpu.VMEM((2, 2, 2, ROWS_A, 128), F32),
        pltpu.VMEM((4, ROWS_A, 128), F32),
    ]

    def direct(rows):
        slabs = pltpu.VMEM((7, 4, rows, 128), CODE)
        return [pltpu.VMEM((4, rows, 128), F32), slabs, slabs, dma((7,)), dma((7,))]

    big = pltpu.VMEM((4, 64, 128), CODE)
    small = pltpu.VMEM((4, 32, 128), CODE)
    messages = [big, big, big, pltpu.VMEM((2, 4, 32, 128), CODE), small, small, small]
    kept = pltpu.VMEM((4, 64, 64), F32)
    tiles = pix_dev // 128
    return pl.pallas_call(
        kernel,
        out_shape=jax.ShapeDtypeStruct((4, 64, 1024), F32),
        in_specs=[
            pl.BlockSpec(memory_space=pltpu.SMEM),
            pl.BlockSpec(memory_space=pltpu.VMEM),
            pl.BlockSpec(memory_space=pltpu.VMEM),
            pl.BlockSpec(memory_space=pltpu.HBM),
        ],
        out_specs=pl.BlockSpec(memory_space=pltpu.VMEM),
        scratch_shapes=[
            pltpu.VMEM((FRAMES_DEV, pix_dev), BF16),
            pltpu.VMEM((tiles, FRAMES_DEV, 128), BF16),
            pltpu.VMEM((tiles, 2 * FRAMES_DEV, 128), BF16),
            pltpu.VMEM((tiles, 2 * FRAMES_DEV, 128), BF16),
            pltpu.VMEM((tiles, FRAMES_DEV, 128), BF16),
            pltpu.VMEM((tiles, FRAMES_DEV, 128), BF16),
            pltpu.VMEM((RELAYED, FRAMES_DEV, 128), BF16),
            pltpu.VMEM((CYCLES, 128), F32),
            pltpu.VMEM((7, CYCLES, 128), F32),
            pltpu.VMEM((CYCLES, 128), F32),
            pltpu.VMEM((5, CYCLES, 128), F32),
            *[pltpu.VMEM((CYCLES, FRAMES_DEV, 128), F32)] * 3,
            *[pltpu.VMEM((CYCLES, 128), F32)] * 3,
            pltpu.VMEM((2, 4, 4, ROWS_A, 128), F32),
            *halves,
            *halves,
            dma((7,)),
            dma((7,)),
            *[ref for rows in DIRECT for ref in direct(rows)],
            *messages,
            *messages,
            kept,
            kept,
            kept,
            dma,
            dma((8,)),
            dma((8,)),
            dma((7,)),
            dma((7,)),
            dma((5,)),
            dma((5,)),
            dma((8,)),
            dma((8,)),
        ],
        compiler_params=pltpu.CompilerParams(
            collective_id=0, has_side_effects=True, vmem_limit_bytes=48 * 2**20
        ),
    )(places, masks, counts, intensity)


def solution(mesh):
    placed = (P("tm", "pix"), P("pix"))
    return jax.shard_map(
        per_device, mesh=mesh, in_specs=placed, out_specs=P("pix", "tm", None), check_vma=False
    )
```

```python
import jax
import jax.numpy as jnp
from jax import lax
from jax.experimental import pallas as pl
from jax.experimental.pallas import tpu as pltpu
from jax.sharding import PartitionSpec as P

CYCLES = 32
CAP = 4
MESH = pl.DeviceIdType.MESH
F32 = jnp.float32
BF16 = jnp.bfloat16
FRAMES_DEV = 64
TOP = 32768.0
STEPS = 2048.0
CODE = jnp.int16
ROWS_A = 64
DIRECT = (64, 96, 64)
RELAYED = 44


def nt(left, right):
    return lax.dot_general(left, right, (((1,), (1,)), ((), ())), preferred_element_type=F32)


def encode(value):
    level = jnp.log2(jnp.maximum(value, 1.0 / 65536.0)) * STEPS
    return jnp.round(level).astype(jnp.int32).astype(CODE)


def decode(code):
    return jnp.exp2(code.astype(jnp.int32).astype(F32) * (1.0 / STEPS))


def fold(block):
    return jnp.concatenate([block[0:32], block[32:64]], axis=1)


def unfold(block):
    return jnp.concatenate([block[:, 0:64], block[:, 64:128]], axis=0)


def kernel(places, masks, counts, x_ref, out_ref, *refs):
    refs = list(refs)

    def take(n):
        got = refs[:n]
        del refs[:n]
        return got

    xv, ownb, obuf, fbuf, y1buf, y2buf, relay = take(7)
    part, landed, tt, tr = take(4)
    col_y1, col_y2, col_f = take(3)
    row_o, row_f, row_2 = take(3)
    set_a = take(9)
    sets = [take(5) for _ in DIRECT]
    s1, s2, s3, s4, s5, s6, s7 = take(7)
    r1, r2, r3, r4, r5, r6, r7 = take(7)
    kept0, kept1, kept2 = take(3)
    own_sem, gs, gr, ps, pr, ts, tsr, fs, fr = take(9)

    tm, pix = lax.axis_index("tm"), lax.axis_index("pix")
    core = tm % 2
    y = (tm // 2) % 4
    kx = tm // 8
    ky = y // 2
    z = pix % 4
    xl = pix // 4
    sib = 1 - core

    def at(k, yy, c):
        return ((k * 4 + yy % 4) * 2 + c, pix)

    def flip(a, b):
        return (a + b) % 2

    k2 = flip(core, ky)
    k1 = flip(core, kx)
    z1 = z + 1 - 2 * (z % 2)
    z3 = 3 - z
    z2 = (z + 2) % 4
    dev_sib = at(kx, y, sib)
    dev_z1 = (tm, xl * 4 + z1)
    dev_z3 = (tm, xl * 4 + z3)
    dev_x = (tm, (1 - xl) * 4 + z)
    near_core = at(kx, y + 1, core)

    own = pltpu.make_async_copy(x_ref, xv, own_sem)
    own.start()
    barrier = pltpu.get_barrier_semaphore()
    friends = [dev_sib] + [(tm, (pix + q) % 8) for q in range(1, 8)]
    for c in range(2):
        friends += [at(kx, y + 1, c), at(kx, y + 3, c), at(kx, y + 2, c), at(1 - kx, y, c)]
    for d in friends:
        pl.semaphore_signal(barrier, inc=1, device_id=d, device_id_type=MESH)
    mine = pl.ds(core * 64, 64)
    own.wait()
    for t in range(x_ref.shape[1] // 128):
        block = xv[:, t * 128 : t * 128 + 128]
        ownb[t] = block
        obuf[t, mine] = block

    def copy(src, dst, ss, rs, d):
        return pltpu.make_async_remote_copy(
            src_ref=src, dst_ref=dst, send_sem=ss, recv_sem=rs, device_id=d, device_id_type=MESH
        )

    def send(src, dst, ss, rs, k, d):
        r = copy(src, dst, ss.at[k], rs.at[k], d)
        r.start()
        return r

    every = pl.ds(0, obuf.shape[0])
    def span(r):
        tile = places[r]
        mask = jnp.broadcast_to(masks[pl.ds(r, 1), :], (8, CAP * 128)).astype(BF16)
        return tile, mask

    def window(ref, tile, rows):
        return jnp.concatenate([ref[tile + k, rows] for k in range(CAP)], axis=1)

    def slot(r):
        return r // 16, (r // 4) % 4, r % 4

    def cycles(body):
        @pl.loop(0, CYCLES, unroll=4)
        def _(r):
            body(r)

    ga = set_a[0]
    whole = slice(None)

    def scaled(r, g, col, rows):
        return g * col * rows[pl.ds(r, 1), :]

    def totals_own(r):
        tile, mask = span(r)
        t = nt(mask, window(ownb, tile, whole))
        part[pl.ds(r, 1)] = jnp.concatenate([t[0:1], counts[pl.ds(r, 1), 0:64]], axis=1)

    def gram_a(r):
        tile, mask = span(r)
        right = window(obuf, tile, whole) * mask[0:1]
        ga[slot(r)] = nt(window(obuf, tile, mine), right)

    def gram_b(r):
        tile, mask = span(r)
        right = window(obuf, tile, whole) * mask[0:1]
        return scaled(r, nt(window(y1buf, tile, whole), right), col_y1[r], row_o)

    def two(tile, mask):
        right = jnp.concatenate([window(obuf, tile, mine), window(fbuf, tile, mine)], axis=0)
        return right * mask[0:1]

    def gram_d(r):
        tile, mask = span(r)
        right = window(fbuf, tile, whole) * mask[0:1]
        first = scaled(r, nt(window(y1buf, tile, whole), right), col_y1[r], row_f)
        fk = pl.ds(k1 * 64, 64)
        right = window(obuf, tile, mine) * mask[0:1]
        g = nt(window(fbuf, tile, fk), right)
        g = g * col_f[r, :, 0:64] * row_2[pl.ds(r, 1), 0:64]
        return jnp.concatenate([first, fold(g)], axis=0)

    def gram_c(r):
        tile, mask = span(r)
        g = nt(window(y2buf, tile, whole), two(tile, mask))
        return scaled(r, g, col_y2[r], row_2)

    lo, hi = pl.ds(0, 2), pl.ds(2, 2)
    both_x = pl.ds(0, 2)

    class Sum:
        def __init__(self, g, e1, e2, e3, r1, r2, r3, ss, rs):
            self.g, self.e, self.r = g, (e1, e2, e3), (r1, r2, r3)
            self.ss, self.rs = ss, rs

        def first(self):
            g, r1 = self.g, self.r[0]
            self.c1 = [
                send(g.at[both_x, z2, lo], r1.at[0, 0], self.ss, self.rs, 0, dev_z1),
                send(g.at[both_x, z2, hi], r1.at[1, 0], self.ss, self.rs, 1, dev_z3),
                send(g.at[both_x, z1, lo], r1.at[0, 1], self.ss, self.rs, 2, dev_z1),
                send(g.at[both_x, z3, hi], r1.at[1, 1], self.ss, self.rs, 3, dev_z3),
            ]

        def second(self):
            g, r1, r2 = self.g, self.r[0], self.r[1]
            self.c2 = []
            for p, (js, zz, d) in enumerate(((0, z3, dev_z3), (2, z1, dev_z1))):
                self.c1[p].wait()
                for i in range(2):
                    for j in range(2):
                        g[i, zz, js + j] += r1[p, 0, i, j]
                self.c2.append(send(g.at[both_x, zz, pl.ds(js, 2)], r2.at[p], self.ss, self.rs, 4 + p, d))
            for p in range(2):
                self.c1[2 + p].wait()
                for i in range(2):
                    for j in range(2):
                        g[i, z, 2 * p + j] += r1[p, 1, i, j]

        def third(self):
            g, r2 = self.g, self.r[1]
            for p in range(2):
                self.c2[p].wait()
                for j in range(2):
                    g[1 - xl, z, 2 * p + j] += r2[p, 1 - xl, j]
            self.c3 = send(g.at[1 - xl, z], self.r[2], self.ss, self.rs, 6, dev_x)
            for p in range(2):
                for j in range(2):
                    g[xl, z, 2 * p + j] += r2[p, xl, j]

        def last(self):
            self.c3.wait()

        def total(self, j):
            return self.g[xl, z, j] + self.r[2][j]

    class Direct:
        def __init__(self, body, own, e, r, ss, rs):
            self.body, self.own, self.e, self.r, self.ss, self.rs = body, own, e, r, ss, rs

        def copy(self, q):
            k = q - 1
            return copy(self.e.at[k], self.r.at[k], self.ss.at[k], self.rs.at[k], (tm, (pix + q) % 8))

        def run(self):
            @pl.loop(1, 8)
            def _(q):
                p = (pix + q) % 8
                for j in range(4):
                    self.e[q - 1, j] = encode(self.body(p * 4 + j))
                self.copy(q).start()

            for j in range(4):
                self.own[j] = self.body(pix * 4 + j)

        def wait(self):
            for q in range(1, 8):
                self.copy(q).wait()

        def total(self, j):
            value = self.own[j]
            for q in range(7):
                value = value + decode(self.r[q, j])
            return value

    sum_a = Sum(*set_a)
    sum_b, sum_d, sum_c = [Direct(body, *q) for body, q in zip((gram_b, gram_d, gram_c), sets)]

    cycles(totals_own)
    pl.semaphore_wait(barrier, len(friends))
    cp = []
    for q in range(1, 8):
        cp.append(send(part, landed.at[q - 1], ps, pr, q - 1, (tm, (pix + q) % 8)))
    pre = pl.ds(0, RELAYED)
    post = pl.ds(RELAYED, obuf.shape[0] - RELAYED)
    dev_prev = at(kx, y + 3, core)
    cp_f = send(ownb, fbuf.at[every, mine], gs, gr, 3, at(1 - kx, y, core))
    cp_y1 = send(ownb, y1buf, gs, gr, 1, dev_prev)
    cp_rel = send(ownb.at[pre], relay, gs, gr, 2, near_core)
    cp_sib = send(ownb, obuf.at[every, mine], gs, gr, 0, dev_sib)
    cp_sib.wait()
    cycles(gram_a)
    sum_a.first()
    total = part[...]
    for q in range(7):
        cp[q].wait()
        total = total + landed[q]
    tt[...] = total
    tcopies = [
        send(tt, tr.at[0], ts, tsr, 0, dev_sib),
        send(tt, tr.at[1], ts, tsr, 1, dev_prev),
        send(tt, tr.at[2], ts, tsr, 2, at(kx, y + 2, flip(core, 1 - ky))),
    ]

    def tcopy(to, slot_core):
        return copy(tt, tr.at[3 + slot_core], ts.at[3 + to], tsr.at[3 + slot_core], at(1 - kx, y, to))

    for c in range(2):
        tcopy(c, core).start()
    sum_a.second()
    cp_rel.wait()
    cp_fr = send(relay, y2buf.at[pre], gs, gr, 7, at(kx, y + 1, flip(core, ((y + 1) % 4) // 2)))
    sum_a.third()
    cp_y1.wait()
    cp_fp = send(y1buf.at[post], y2buf.at[post], gs, gr, 6, at(kx, y + 3, flip(core, ((y + 3) % 4) // 2)))
    for c in tcopies:
        c.wait()
    for c in range(2):
        tcopy(c, core).wait_send()
        tcopy(c, c).wait_recv()

    def pair(first, second):
        return 1.0 / jnp.concatenate([first[:, 0:64], second[:, 0:64]], axis=1)

    def fill(col, table):
        up = (TOP / table.T)[0:64]
        for r in range(CYCLES):
            col[r] = jnp.broadcast_to(up[:, r : r + 1], (64, 128))

    mine_t, sib_t, f0_t, f1_t = tt[...], tr[0], tr[3], tr[4]
    row_o[...] = jnp.where(core == 0, pair(mine_t, sib_t), pair(sib_t, mine_t))
    row_f[...] = pair(f0_t, f1_t)
    row_2[...] = pair(mine_t, jnp.where(core == 0, f0_t, f1_t))
    fill(col_y1, tr[1])

    here = kx * 4 + y
    near = kx * 4 + (y + 1) % 4
    prev = kx * 4 + (y + 3) % 4
    opp = kx * 4 + (y + 2) % 4
    cross = (1 - kx) * 4 + y
    cross_near = (1 - kx) * 4 + (y + 1) % 4
    cross_prev = (1 - kx) * 4 + (y + 3) % 4
    cross_opp = (1 - kx) * 4 + (y + 2) % 4

    def place(j, chip, value):
        value = value * (count(j) * (1.0 / TOP))
        out_ref[j, :, pl.ds(pl.multiple_of(chip * 128, 128), 128)] = value

    def ordered(k, local, remote):
        first = jnp.where(k == 0, local, remote)
        second = jnp.where(k == 0, remote, local)
        return jnp.concatenate([first, second], axis=1)

    def count(j):
        return tt[pl.ds(pix * 4 + j, 1), 64:65]

    def final_a():
        for j in range(4):
            lanes = row_o[pl.ds(pix * 4 + j, 1), :]
            up = (TOP / jnp.broadcast_to(tt[pl.ds(pix * 4 + j, 1), :], (8, 128)).T)[0:64, 0:1]
            place(j, here, sum_a.total(j) * up * lanes)

    def final_b():
        for j in range(4):
            b = sum_b.total(j)
            s1[j] = encode(b)
            bt = b.T
            kept0[j] = jnp.where(core == 0, bt[0:64], bt[64:128])
            s7[j] = encode(fold(jnp.where(core == 0, bt[64:128], bt[0:64])))
        return [
            send(s1, r1, fs, fr, 0, near_core),
            send(s7, r7, fs, fr, 1, dev_sib),
        ]

    def copy4(to, landing):
        return copy(s4.at[to], r4.at[landing], fs.at[2 + to], fr.at[2 + landing], at(1 - kx, y, to))

    def final_d():
        for j in range(4):
            g = sum_d.total(j)
            s2[j] = encode(g[0:64])
            dt = g[0:64].T
            s4[0, j] = encode(fold(dt[0:64]))
            s4[1, j] = encode(fold(dt[64:128]))
            s6[j] = encode(g[64:96])
            kept1[j] = unfold(g[64:96]).T
        for c in range(2):
            copy4(c, core).start()
        return [
            send(s2, r2, fs, fr, 4, near_core),
            send(s6, r6, fs, fr, 5, at(1 - kx, y, k1)),
        ]

    def final_c():
        for j in range(4):
            e = sum_c.total(j)
            s3[j] = encode(e)
            et = e.T
            kept2[j] = et[0:64]
            s5[j] = encode(fold(et[64:128]))
        return [
            send(s3, r3, fs, fr, 6, at(kx, y + 2, k2)),
            send(s5, r5, fs, fr, 7, at(1 - kx, y, core)),
        ]

    cp_f.wait()
    fw_f = send(fbuf.at[every, mine], fbuf.at[every, mine], gs, gr, 4, dev_sib)
    sum_b.run()
    fill(col_f, jnp.where(k1 == 0, f0_t, f1_t))
    fw_f.wait()
    sum_d.run()
    fill(col_y2, tr[2])
    cp_fp.wait()
    cp_fr.wait()
    sum_c.run()
    sum_a.last()
    final_a()
    sum_b.wait()
    out_b = final_b()
    sum_d.wait()
    out_d = final_d()
    sum_c.wait()
    out_c = final_c()
    for c in out_b:
        c.wait()
    for j in range(4):
        place(j, near, ordered(core, kept0[j], unfold(decode(r7[j]))))
        place(j, prev, decode(r1[j]))

    for c in range(2):
        copy4(c, core).wait_send()
        copy4(c, c).wait_recv()
    for c in out_d:
        c.wait()
    for j in range(4):
        place(j, cross_near, jnp.concatenate([unfold(decode(r4[0, j])), unfold(decode(r4[1, j]))], axis=1))
        place(j, cross_prev, decode(r2[j]))
        place(j, cross, ordered(k1, kept1[j], unfold(decode(r6[j]))))
    for c in out_c:
        c.wait()
    for j in range(4):
        far = decode(r3[j])
        place(j, opp, ordered(k2, kept2[j], far[:, 0:64]))
        place(j, cross_opp, ordered(k2, unfold(decode(r5[j])), far[:, 64:128]))


def per_device(intensity, labels):
    tile_lab = labels.reshape(-1, 128)[:, 0]
    cycles = jnp.arange(CYCLES, dtype=jnp.int32)
    first = jnp.sum((tile_lab[None, :] < cycles[:, None]).astype(jnp.int32), axis=1)
    count = jnp.sum((tile_lab[None, :] == cycles[:, None]).astype(jnp.int32), axis=1)
    places = jnp.minimum(first, tile_lab.shape[0] - CAP)
    low = (first - places) * 128
    high = low + count * 128
    lane = jnp.arange(CAP * 128, dtype=jnp.int32)[None, :]
    masks = ((lane >= low[:, None]) & (lane < high[:, None])).astype(F32)
    counts = jnp.broadcast_to((count * 128).astype(F32)[:, None], (CYCLES, 128))
    pix_dev = intensity.shape[1]
    dma = pltpu.SemaphoreType.DMA

    halves = [
        pltpu.VMEM((2, 2, 2, 2, ROWS_A, 128), F32),
        pltpu.VMEM((2, 2, 2, ROWS_A, 128), F32),
        pltpu.VMEM((4, ROWS_A, 128), F32),
    ]

    def direct(rows):
        slabs = pltpu.VMEM((7, 4, rows, 128), CODE)
        return [pltpu.VMEM((4, rows, 128), F32), slabs, slabs, dma((7,)), dma((7,))]

    big = pltpu.VMEM((4, 64, 128), CODE)
    small = pltpu.VMEM((4, 32, 128), CODE)
    messages = [big, big, big, pltpu.VMEM((2, 4, 32, 128), CODE), small, small, small]
    kept = pltpu.VMEM((4, 64, 64), F32)
    tiles = pix_dev // 128
    return pl.pallas_call(
        kernel,
        out_shape=jax.ShapeDtypeStruct((4, 64, 1024), F32),
        in_specs=[
            pl.BlockSpec(memory_space=pltpu.SMEM),
            pl.BlockSpec(memory_space=pltpu.VMEM),
            pl.BlockSpec(memory_space=pltpu.VMEM),
            pl.BlockSpec(memory_space=pltpu.HBM),
        ],
        out_specs=pl.BlockSpec(memory_space=pltpu.VMEM),
        scratch_shapes=[
            pltpu.VMEM((FRAMES_DEV, pix_dev), BF16),
            pltpu.VMEM((tiles, FRAMES_DEV, 128), BF16),
            pltpu.VMEM((tiles, 2 * FRAMES_DEV, 128), BF16),
            pltpu.VMEM((tiles, 2 * FRAMES_DEV, 128), BF16),
            pltpu.VMEM((tiles, FRAMES_DEV, 128), BF16),
            pltpu.VMEM((tiles, FRAMES_DEV, 128), BF16),
            pltpu.VMEM((RELAYED, FRAMES_DEV, 128), BF16),
            pltpu.VMEM((CYCLES, 128), F32),
            pltpu.VMEM((7, CYCLES, 128), F32),
            pltpu.VMEM((CYCLES, 128), F32),
            pltpu.VMEM((5, CYCLES, 128), F32),
            *[pltpu.VMEM((CYCLES, FRAMES_DEV, 128), F32)] * 3,
            *[pltpu.VMEM((CYCLES, 128), F32)] * 3,
            pltpu.VMEM((2, 4, 4, ROWS_A, 128), F32),
            *halves,
            *halves,
            dma((7,)),
            dma((7,)),
            *[ref for rows in DIRECT for ref in direct(rows)],
            *messages,
            *messages,
            kept,
            kept,
            kept,
            dma,
            dma((8,)),
            dma((8,)),
            dma((7,)),
            dma((7,)),
            dma((5,)),
            dma((5,)),
            dma((8,)),
            dma((8,)),
        ],
        compiler_params=pltpu.CompilerParams(
            collective_id=0, has_side_effects=True, vmem_limit_bytes=48 * 2**20
        ),
    )(places, masks, counts, intensity)


def solution(mesh):
    placed = (P("tm", "pix"), P("pix"))
    return jax.shard_map(
        per_device, mesh=mesh, in_specs=placed, out_specs=P("pix", "tm", None), check_vma=False
    )
```

```python
import jax
import jax.numpy as jnp
from jax import lax
from jax.experimental import pallas as pl
from jax.experimental.pallas import tpu as pltpu
from jax.sharding import PartitionSpec as P

CYCLES = 32
CAP = 4
MESH = pl.DeviceIdType.MESH
F32 = jnp.float32
BF16 = jnp.bfloat16
FRAMES_DEV = 64
TOP = 32768.0
STEPS = 2048.0
CODE = jnp.int16
ROWS_A = 64
MIXED = (64, 96)
DIRECT = 64
RELAYED = 44


def nt(left, right):
    return lax.dot_general(left, right, (((1,), (1,)), ((), ())), preferred_element_type=F32)


def encode(value):
    level = jnp.log2(jnp.maximum(value, 1.0 / 65536.0)) * STEPS
    return jnp.round(level).astype(jnp.int32).astype(CODE)


def decode(code):
    return jnp.exp2(code.astype(jnp.int32).astype(F32) * (1.0 / STEPS))


def fold(block):
    return jnp.concatenate([block[0:32], block[32:64]], axis=1)


def unfold(block):
    return jnp.concatenate([block[:, 0:64], block[:, 64:128]], axis=0)


def kernel(places, masks, counts, x_ref, out_ref, *refs):
    refs = list(refs)

    def take(n):
        got = refs[:n]
        del refs[:n]
        return got

    xv, ownb, obuf, fbuf, y1buf, y2buf, relay = take(7)
    part, landed, tt, tr = take(4)
    col_y1, col_y2, col_f = take(3)
    row_o, row_f, row_2 = take(3)
    set_a = take(9)
    mixed = [take(12) for _ in MIXED]
    set_c = take(5)
    s1, s2, s3, s4, s5, s6, s7 = take(7)
    r1, r2, r3, r4, r5, r6, r7 = take(7)
    kept0, kept1, kept2 = take(3)
    own_sem, gs, gr, ps, pr, ts, tsr, fs, fr = take(9)

    tm, pix = lax.axis_index("tm"), lax.axis_index("pix")
    core = tm % 2
    y = (tm // 2) % 4
    kx = tm // 8
    ky = y // 2
    z = pix % 4
    xl = pix // 4
    sib = 1 - core

    def at(k, yy, c):
        return ((k * 4 + yy % 4) * 2 + c, pix)

    def flip(a, b):
        return (a + b) % 2

    k2 = flip(core, ky)
    k1 = flip(core, kx)
    z1 = z + 1 - 2 * (z % 2)
    z3 = 3 - z
    z2 = (z + 2) % 4
    dev_sib = at(kx, y, sib)
    dev_z1 = (tm, xl * 4 + z1)
    dev_z3 = (tm, xl * 4 + z3)
    dev_x = (tm, (1 - xl) * 4 + z)
    near_core = at(kx, y + 1, core)

    own = pltpu.make_async_copy(x_ref, xv, own_sem)
    own.start()
    barrier = pltpu.get_barrier_semaphore()
    friends = [dev_sib] + [(tm, (pix + q) % 8) for q in range(1, 8)]
    for c in range(2):
        friends += [at(kx, y + 1, c), at(kx, y + 3, c), at(kx, y + 2, c), at(1 - kx, y, c)]
    for d in friends:
        pl.semaphore_signal(barrier, inc=1, device_id=d, device_id_type=MESH)
    mine = pl.ds(core * 64, 64)
    own.wait()
    for t in range(x_ref.shape[1] // 128):
        block = xv[:, t * 128 : t * 128 + 128]
        ownb[t] = block
        obuf[t, mine] = block

    def copy(src, dst, ss, rs, d):
        return pltpu.make_async_remote_copy(
            src_ref=src, dst_ref=dst, send_sem=ss, recv_sem=rs, device_id=d, device_id_type=MESH
        )

    def send(src, dst, ss, rs, k, d):
        r = copy(src, dst, ss.at[k], rs.at[k], d)
        r.start()
        return r

    every = pl.ds(0, obuf.shape[0])
    def span(r):
        tile = places[r]
        mask = jnp.broadcast_to(masks[pl.ds(r, 1), :], (8, CAP * 128)).astype(BF16)
        return tile, mask

    def window(ref, tile, rows):
        return jnp.concatenate([ref[tile + k, rows] for k in range(CAP)], axis=1)

    def slot(r):
        return r // 16, (r // 4) % 4, r % 4

    def cycles(body):
        @pl.loop(0, CYCLES, unroll=4)
        def _(r):
            body(r)

    ga = set_a[0]
    whole = slice(None)

    def scaled(r, g, col, rows):
        return g * col * rows[pl.ds(r, 1), :]

    def totals_own(r):
        tile, mask = span(r)
        t = nt(mask, window(ownb, tile, whole))
        part[pl.ds(r, 1)] = jnp.concatenate([t[0:1], counts[pl.ds(r, 1), 0:64]], axis=1)

    def gram_a(r):
        tile, mask = span(r)
        right = window(obuf, tile, whole) * mask[0:1]
        ga[slot(r)] = nt(window(obuf, tile, mine), right)

    def gram_b(r):
        tile, mask = span(r)
        right = window(obuf, tile, whole) * mask[0:1]
        return scaled(r, nt(window(y1buf, tile, whole), right), col_y1[r], row_o)

    def two(tile, mask):
        right = jnp.concatenate([window(obuf, tile, mine), window(fbuf, tile, mine)], axis=0)
        return right * mask[0:1]

    def gram_d(r):
        tile, mask = span(r)
        right = window(fbuf, tile, whole) * mask[0:1]
        first = scaled(r, nt(window(y1buf, tile, whole), right), col_y1[r], row_f)
        fk = pl.ds(k1 * 64, 64)
        right = window(obuf, tile, mine) * mask[0:1]
        g = nt(window(fbuf, tile, fk), right)
        g = g * col_f[r, :, 0:64] * row_2[pl.ds(r, 1), 0:64]
        return jnp.concatenate([first, fold(g)], axis=0)

    def gram_c(r):
        tile, mask = span(r)
        g = nt(window(y2buf, tile, whole), two(tile, mask))
        return scaled(r, g, col_y2[r], row_2)

    lo, hi = pl.ds(0, 2), pl.ds(2, 2)
    both_x = pl.ds(0, 2)

    class Sum:
        def __init__(self, g, e1, e2, e3, r1, r2, r3, ss, rs):
            self.g, self.e, self.r = g, (e1, e2, e3), (r1, r2, r3)
            self.ss, self.rs = ss, rs

        def first(self):
            g, r1 = self.g, self.r[0]
            self.c1 = [
                send(g.at[both_x, z2, lo], r1.at[0, 0], self.ss, self.rs, 0, dev_z1),
                send(g.at[both_x, z2, hi], r1.at[1, 0], self.ss, self.rs, 1, dev_z3),
                send(g.at[both_x, z1, lo], r1.at[0, 1], self.ss, self.rs, 2, dev_z1),
                send(g.at[both_x, z3, hi], r1.at[1, 1], self.ss, self.rs, 3, dev_z3),
            ]

        def second(self):
            g, r1, r2 = self.g, self.r[0], self.r[1]
            self.c2 = []
            for p, (js, zz, d) in enumerate(((0, z3, dev_z3), (2, z1, dev_z1))):
                self.c1[p].wait()
                for i in range(2):
                    for j in range(2):
                        g[i, zz, js + j] += r1[p, 0, i, j]
                self.c2.append(send(g.at[both_x, zz, pl.ds(js, 2)], r2.at[p], self.ss, self.rs, 4 + p, d))
            for p in range(2):
                self.c1[2 + p].wait()
                for i in range(2):
                    for j in range(2):
                        g[i, z, 2 * p + j] += r1[p, 1, i, j]

        def third(self):
            g, r2 = self.g, self.r[1]
            for p in range(2):
                self.c2[p].wait()
                for j in range(2):
                    g[1 - xl, z, 2 * p + j] += r2[p, 1 - xl, j]
            self.c3 = send(g.at[1 - xl, z], self.r[2], self.ss, self.rs, 6, dev_x)
            for p in range(2):
                for j in range(2):
                    g[xl, z, 2 * p + j] += r2[p, xl, j]

        def last(self):
            self.c3.wait()

        def total(self, j):
            return self.g[xl, z, j] + self.r[2][j]

    class Direct:
        def __init__(self, body, own, e, r, ss, rs):
            self.body, self.own, self.e, self.r, self.ss, self.rs = body, own, e, r, ss, rs

        def copy(self, q):
            k = q - 1
            return copy(self.e.at[k], self.r.at[k], self.ss.at[k], self.rs.at[k], (tm, (pix + q) % 8))

        def run(self):
            @pl.loop(1, 8)
            def _(q):
                p = (pix + q) % 8
                for j in range(4):
                    self.e[q - 1, j] = encode(self.body(p * 4 + j))
                self.copy(q).start()

            for j in range(4):
                self.own[j] = self.body(pix * 4 + j)

        def wait(self):
            for q in range(1, 8):
                self.copy(q).wait()

        def total(self, j):
            value = self.own[j]
            for q in range(7):
                value = value + decode(self.r[q, j])
            return value

    sum_a = Sum(*set_a)
    class Mixed:
        def __init__(self, body, keepx, keepz, ex, ez, e2x, e2z, rx, rz, r2x, r2z, ss, rs):
            self.body, self.keepx, self.keepz = body, keepx, keepz
            self.ex, self.ez, self.e2x, self.e2z = ex, ez, e2x, e2z
            self.rx, self.rz, self.r2x, self.r2z = rx, rz, r2x, r2z
            self.ss, self.rs = ss, rs

        def go(self, src, dst, k, d):
            return copy(src, dst, self.ss.at[k], self.rs.at[k], d)

        def x_first(self, k):
            return self.go(self.ex.at[k], self.rx.at[k], k, dev_x)

        def z_first(self, q):
            d = (tm, xl * 4 + (z + q) % 4)
            return self.go(self.ez.at[q - 1], self.rz.at[q - 1], 3 + q, d)

        def z_second(self, q):
            d = (tm, xl * 4 + (z + q) % 4)
            return self.go(self.e2x.at[q - 1], self.r2x.at[q - 1], 6 + q, d)

        def x_second(self):
            return self.go(self.e2z, self.r2z, 10, dev_x)

        def run(self):
            @pl.loop(0, 4)
            def _(k):
                for j in range(2):
                    self.ex[k, j] = encode(self.body(((1 - xl) * 4 + k) * 4 + j))
                self.x_first(k).start()

            @pl.loop(1, 4)
            def _(q):
                for i in range(2):
                    for j in range(2):
                        value = self.body((i * 4 + (z + q) % 4) * 4 + 2 + j)
                        self.ez[q - 1, i, j] = encode(value)
                self.z_first(q).start()

            @pl.loop(0, 4)
            def _(k):
                for j in range(2):
                    self.keepx[k, j] = self.body((xl * 4 + k) * 4 + j)

            @pl.loop(0, 2)
            def _(i):
                for j in range(2):
                    self.keepz[i, j] = self.body((i * 4 + z) * 4 + 2 + j)

        def mid(self):
            for k in range(4):
                self.x_first(k).wait()
            for q in range(1, 4):
                k = (z + q) % 4
                for j in range(2):
                    self.e2x[q - 1, j] = encode(self.keepx[k, j] + decode(self.rx[k, j]))
                self.z_second(q).start()
            for q in range(1, 4):
                self.z_first(q).wait()
            for j in range(2):
                self.e2z[j] = encode(self.over_z(1 - xl, j))
            self.x_second().start()

        def over_z(self, i, j):
            value = self.keepz[i, j]
            for q in range(3):
                value = value + decode(self.rz[q, i, j])
            return value

        def wait(self):
            for q in range(1, 4):
                self.z_second(q).wait()
            self.x_second().wait()

        def total(self, j):
            if j < 2:
                value = self.keepx[z, j] + decode(self.rx[z, j])
                for q in range(3):
                    value = value + decode(self.r2x[q, j])
                return value
            return self.over_z(xl, j - 2) + decode(self.r2z[j - 2])

    sum_b, sum_d = Mixed(gram_b, *mixed[0]), Mixed(gram_d, *mixed[1])
    sum_c = Direct(gram_c, *set_c)

    cycles(totals_own)
    pl.semaphore_wait(barrier, len(friends))
    cp = []
    for q in range(1, 8):
        cp.append(send(part, landed.at[q - 1], ps, pr, q - 1, (tm, (pix + q) % 8)))
    pre = pl.ds(0, RELAYED)
    post = pl.ds(RELAYED, obuf.shape[0] - RELAYED)
    dev_prev = at(kx, y + 3, core)
    cp_f = send(ownb, fbuf.at[every, mine], gs, gr, 3, at(1 - kx, y, core))
    cp_y1 = send(ownb, y1buf, gs, gr, 1, dev_prev)
    cp_rel = send(ownb.at[pre], relay, gs, gr, 2, near_core)
    cp_sib = send(ownb, obuf.at[every, mine], gs, gr, 0, dev_sib)
    cp_sib.wait()
    cycles(gram_a)
    sum_a.first()
    total = part[...]
    for q in range(7):
        cp[q].wait()
        total = total + landed[q]
    tt[...] = total
    tcopies = [
        send(tt, tr.at[0], ts, tsr, 0, dev_sib),
        send(tt, tr.at[1], ts, tsr, 1, dev_prev),
        send(tt, tr.at[2], ts, tsr, 2, at(kx, y + 2, flip(core, 1 - ky))),
    ]

    def tcopy(to, slot_core):
        return copy(tt, tr.at[3 + slot_core], ts.at[3 + to], tsr.at[3 + slot_core], at(1 - kx, y, to))

    for c in range(2):
        tcopy(c, core).start()
    sum_a.second()
    cp_rel.wait()
    cp_fr = send(relay, y2buf.at[pre], gs, gr, 7, at(kx, y + 1, flip(core, ((y + 1) % 4) // 2)))
    cp_y1.wait()
    cp_fp = send(y1buf.at[post], y2buf.at[post], gs, gr, 6, at(kx, y + 3, flip(core, ((y + 3) % 4) // 2)))
    for c in tcopies:
        c.wait()
    for c in range(2):
        tcopy(c, core).wait_send()
        tcopy(c, c).wait_recv()

    def pair(first, second):
        return 1.0 / jnp.concatenate([first[:, 0:64], second[:, 0:64]], axis=1)

    def fill(col, table):
        up = (TOP / table.T)[0:64]
        for r in range(CYCLES):
            col[r] = jnp.broadcast_to(up[:, r : r + 1], (64, 128))

    mine_t, sib_t, f0_t, f1_t = tt[...], tr[0], tr[3], tr[4]
    row_o[...] = jnp.where(core == 0, pair(mine_t, sib_t), pair(sib_t, mine_t))
    row_f[...] = pair(f0_t, f1_t)
    row_2[...] = pair(mine_t, jnp.where(core == 0, f0_t, f1_t))
    fill(col_y1, tr[1])

    here = kx * 4 + y
    near = kx * 4 + (y + 1) % 4
    prev = kx * 4 + (y + 3) % 4
    opp = kx * 4 + (y + 2) % 4
    cross = (1 - kx) * 4 + y
    cross_near = (1 - kx) * 4 + (y + 1) % 4
    cross_prev = (1 - kx) * 4 + (y + 3) % 4
    cross_opp = (1 - kx) * 4 + (y + 2) % 4

    def place(j, chip, value):
        value = value * (count(j) * (1.0 / TOP))
        out_ref[j, :, pl.ds(pl.multiple_of(chip * 128, 128), 128)] = value

    def ordered(k, local, remote):
        first = jnp.where(k == 0, local, remote)
        second = jnp.where(k == 0, remote, local)
        return jnp.concatenate([first, second], axis=1)

    def count(j):
        return tt[pl.ds(pix * 4 + j, 1), 64:65]

    def final_a():
        for j in range(4):
            lanes = row_o[pl.ds(pix * 4 + j, 1), :]
            up = (TOP / jnp.broadcast_to(tt[pl.ds(pix * 4 + j, 1), :], (8, 128)).T)[0:64, 0:1]
            place(j, here, sum_a.total(j) * up * lanes)

    def final_b():
        for j in range(4):
            b = sum_b.total(j)
            s1[j] = encode(b)
            bt = b.T
            kept0[j] = jnp.where(core == 0, bt[0:64], bt[64:128])
            s7[j] = encode(fold(jnp.where(core == 0, bt[64:128], bt[0:64])))
        return [
            send(s1, r1, fs, fr, 0, near_core),
            send(s7, r7, fs, fr, 1, dev_sib),
        ]

    def copy4(to, landing):
        return copy(s4.at[to], r4.at[landing], fs.at[2 + to], fr.at[2 + landing], at(1 - kx, y, to))

    def final_d():
        for j in range(4):
            g = sum_d.total(j)
            s2[j] = encode(g[0:64])
            dt = g[0:64].T
            s4[0, j] = encode(fold(dt[0:64]))
            s4[1, j] = encode(fold(dt[64:128]))
            s6[j] = encode(g[64:96])
            kept1[j] = unfold(g[64:96]).T
        for c in range(2):
            copy4(c, core).start()
        return [
            send(s2, r2, fs, fr, 4, near_core),
            send(s6, r6, fs, fr, 5, at(1 - kx, y, k1)),
        ]

    def final_c():
        for j in range(4):
            e = sum_c.total(j)
            s3[j] = encode(e)
            et = e.T
            kept2[j] = et[0:64]
            s5[j] = encode(fold(et[64:128]))
        return [
            send(s3, r3, fs, fr, 6, at(kx, y + 2, k2)),
            send(s5, r5, fs, fr, 7, at(1 - kx, y, core)),
        ]

    cp_f.wait()
    fw_f = send(fbuf.at[every, mine], fbuf.at[every, mine], gs, gr, 4, dev_sib)
    sum_b.run()
    fill(col_f, jnp.where(k1 == 0, f0_t, f1_t))
    fw_f.wait()
    sum_d.run()
    sum_a.third()
    sum_b.mid()
    fill(col_y2, tr[2])
    cp_fp.wait()
    cp_fr.wait()
    sum_c.run()
    sum_d.mid()
    sum_a.last()
    final_a()
    sum_b.wait()
    out_b = final_b()
    sum_d.wait()
    out_d = final_d()
    sum_c.wait()
    out_c = final_c()
    for c in out_b:
        c.wait()
    for j in range(4):
        place(j, near, ordered(core, kept0[j], unfold(decode(r7[j]))))
        place(j, prev, decode(r1[j]))

    for c in range(2):
        copy4(c, core).wait_send()
        copy4(c, c).wait_recv()
    for c in out_d:
        c.wait()
    for j in range(4):
        place(j, cross_near, jnp.concatenate([unfold(decode(r4[0, j])), unfold(decode(r4[1, j]))], axis=1))
        place(j, cross_prev, decode(r2[j]))
        place(j, cross, ordered(k1, kept1[j], unfold(decode(r6[j]))))
    for c in out_c:
        c.wait()
    for j in range(4):
        far = decode(r3[j])
        place(j, opp, ordered(k2, kept2[j], far[:, 0:64]))
        place(j, cross_opp, ordered(k2, unfold(decode(r5[j])), far[:, 64:128]))


def per_device(intensity, labels):
    tile_lab = labels.reshape(-1, 128)[:, 0]
    cycles = jnp.arange(CYCLES, dtype=jnp.int32)
    first = jnp.sum((tile_lab[None, :] < cycles[:, None]).astype(jnp.int32), axis=1)
    count = jnp.sum((tile_lab[None, :] == cycles[:, None]).astype(jnp.int32), axis=1)
    places = jnp.minimum(first, tile_lab.shape[0] - CAP)
    low = (first - places) * 128
    high = low + count * 128
    lane = jnp.arange(CAP * 128, dtype=jnp.int32)[None, :]
    masks = ((lane >= low[:, None]) & (lane < high[:, None])).astype(F32)
    counts = jnp.broadcast_to((count * 128).astype(F32)[:, None], (CYCLES, 128))
    pix_dev = intensity.shape[1]
    dma = pltpu.SemaphoreType.DMA

    halves = [
        pltpu.VMEM((2, 2, 2, 2, ROWS_A, 128), F32),
        pltpu.VMEM((2, 2, 2, ROWS_A, 128), F32),
        pltpu.VMEM((4, ROWS_A, 128), F32),
    ]

    def two_ways(rows):
        def codes(*lead):
            return pltpu.VMEM((*lead, rows, 128), CODE)

        moved = [codes(4, 2), codes(3, 2, 2), codes(3, 2), codes(2)]
        kept = [pltpu.VMEM((4, 2, rows, 128), F32), pltpu.VMEM((2, 2, rows, 128), F32)]
        return [*kept, *moved, *moved, dma((11,)), dma((11,))]

    def direct(rows):
        slabs = pltpu.VMEM((7, 4, rows, 128), CODE)
        return [pltpu.VMEM((4, rows, 128), F32), slabs, slabs, dma((7,)), dma((7,))]

    big = pltpu.VMEM((4, 64, 128), CODE)
    small = pltpu.VMEM((4, 32, 128), CODE)
    messages = [big, big, big, pltpu.VMEM((2, 4, 32, 128), CODE), small, small, small]
    kept = pltpu.VMEM((4, 64, 64), F32)
    tiles = pix_dev // 128
    return pl.pallas_call(
        kernel,
        out_shape=jax.ShapeDtypeStruct((4, 64, 1024), F32),
        in_specs=[
            pl.BlockSpec(memory_space=pltpu.SMEM),
            pl.BlockSpec(memory_space=pltpu.VMEM),
            pl.BlockSpec(memory_space=pltpu.VMEM),
            pl.BlockSpec(memory_space=pltpu.HBM),
        ],
        out_specs=pl.BlockSpec(memory_space=pltpu.VMEM),
        scratch_shapes=[
            pltpu.VMEM((FRAMES_DEV, pix_dev), BF16),
            pltpu.VMEM((tiles, FRAMES_DEV, 128), BF16),
            pltpu.VMEM((tiles, 2 * FRAMES_DEV, 128), BF16),
            pltpu.VMEM((tiles, 2 * FRAMES_DEV, 128), BF16),
            pltpu.VMEM((tiles, FRAMES_DEV, 128), BF16),
            pltpu.VMEM((tiles, FRAMES_DEV, 128), BF16),
            pltpu.VMEM((RELAYED, FRAMES_DEV, 128), BF16),
            pltpu.VMEM((CYCLES, 128), F32),
            pltpu.VMEM((7, CYCLES, 128), F32),
            pltpu.VMEM((CYCLES, 128), F32),
            pltpu.VMEM((5, CYCLES, 128), F32),
            *[pltpu.VMEM((CYCLES, FRAMES_DEV, 128), F32)] * 3,
            *[pltpu.VMEM((CYCLES, 128), F32)] * 3,
            pltpu.VMEM((2, 4, 4, ROWS_A, 128), F32),
            *halves,
            *halves,
            dma((7,)),
            dma((7,)),
            *[ref for rows in MIXED for ref in two_ways(rows)],
            *direct(DIRECT),
            *messages,
            *messages,
            kept,
            kept,
            kept,
            dma,
            dma((8,)),
            dma((8,)),
            dma((7,)),
            dma((7,)),
            dma((5,)),
            dma((5,)),
            dma((8,)),
            dma((8,)),
        ],
        compiler_params=pltpu.CompilerParams(
            collective_id=0, has_side_effects=True, vmem_limit_bytes=48 * 2**20
        ),
    )(places, masks, counts, intensity)


def solution(mesh):
    placed = (P("tm", "pix"), P("pix"))
    return jax.shard_map(
        per_device, mesh=mesh, in_specs=placed, out_specs=P("pix", "tm", None), check_vma=False
    )
```

```python
import jax
import jax.numpy as jnp
from jax import lax
from jax.experimental import pallas as pl
from jax.experimental.pallas import tpu as pltpu
from jax.sharding import PartitionSpec as P

CYCLES = 32
CAP = 4
MESH = pl.DeviceIdType.MESH
F32 = jnp.float32
BF16 = jnp.bfloat16
FRAMES_DEV = 64
TOP = 32768.0
STEPS = 2048.0
CODE = jnp.int16
ROWS_A = 64
MIXED = (64, 96)
DIRECT = 64
RELAYED = 44


def nt(left, right):
    return lax.dot_general(left, right, (((1,), (1,)), ((), ())), preferred_element_type=F32)


def encode(value):
    level = jnp.log2(jnp.maximum(value, 1.0 / 65536.0)) * STEPS
    return jnp.round(level).astype(jnp.int32).astype(CODE)


def decode(code):
    return jnp.exp2(code.astype(jnp.int32).astype(F32) * (1.0 / STEPS))


def fold(block):
    return jnp.concatenate([block[0:32], block[32:64]], axis=1)


def unfold(block):
    return jnp.concatenate([block[:, 0:64], block[:, 64:128]], axis=0)


def kernel(places, masks, counts, x_ref, out_ref, *refs):
    refs = list(refs)

    def take(n):
        got = refs[:n]
        del refs[:n]
        return got

    xv, ownb, obuf, fbuf, y1buf, y2buf, relay = take(7)
    part, landed, tt, tr = take(4)
    col_y1, col_y2, col_f = take(3)
    row_o, row_f, row_2 = take(3)
    set_a = take(9)
    mixed = [take(12) for _ in MIXED]
    set_c = take(5)
    s1, s2, s3, s4, s5, s6, s7 = take(7)
    r1, r2, r3, r4, r5, r6, r7 = take(7)
    kept0, kept1, kept2 = take(3)
    own_sem, gs, gr, ps, pr, ts, tsr, fs, fr = take(9)

    tm, pix = lax.axis_index("tm"), lax.axis_index("pix")
    core = tm % 2
    y = (tm // 2) % 4
    kx = tm // 8
    ky = y // 2
    z = pix % 4
    xl = pix // 4
    sib = 1 - core

    def at(k, yy, c):
        return ((k * 4 + yy % 4) * 2 + c, pix)

    def flip(a, b):
        return (a + b) % 2

    k2 = flip(core, ky)
    k1 = flip(core, kx)
    z1 = z + 1 - 2 * (z % 2)
    z3 = 3 - z
    z2 = (z + 2) % 4
    dev_sib = at(kx, y, sib)
    dev_z1 = (tm, xl * 4 + z1)
    dev_z3 = (tm, xl * 4 + z3)
    dev_x = (tm, (1 - xl) * 4 + z)
    near_core = at(kx, y + 1, core)

    own = pltpu.make_async_copy(x_ref, xv, own_sem)
    own.start()
    barrier = pltpu.get_barrier_semaphore()
    friends = [dev_sib] + [(tm, (pix + q) % 8) for q in range(1, 8)]
    for c in range(2):
        friends += [at(kx, y + 1, c), at(kx, y + 3, c), at(kx, y + 2, c), at(1 - kx, y, c)]
    for d in friends:
        pl.semaphore_signal(barrier, inc=1, device_id=d, device_id_type=MESH)
    mine = pl.ds(core * 64, 64)
    own.wait()
    for t in range(x_ref.shape[1] // 128):
        block = xv[:, t * 128 : t * 128 + 128]
        ownb[t] = block
        obuf[t, mine] = block

    def copy(src, dst, ss, rs, d):
        return pltpu.make_async_remote_copy(
            src_ref=src, dst_ref=dst, send_sem=ss, recv_sem=rs, device_id=d, device_id_type=MESH
        )

    def send(src, dst, ss, rs, k, d):
        r = copy(src, dst, ss.at[k], rs.at[k], d)
        r.start()
        return r

    every = pl.ds(0, obuf.shape[0])
    def span(r):
        tile = places[r]
        mask = jnp.broadcast_to(masks[pl.ds(r, 1), :], (8, CAP * 128)).astype(BF16)
        return tile, mask

    def window(ref, tile, rows):
        return jnp.concatenate([ref[tile + k, rows] for k in range(CAP)], axis=1)

    def slot(r):
        return r // 16, (r // 4) % 4, r % 4

    def cycles(body):
        @pl.loop(0, CYCLES, unroll=4)
        def _(r):
            body(r)

    ga = set_a[0]
    whole = slice(None)

    def scaled(r, g, col, rows):
        return g * col * rows[pl.ds(r, 1), :]

    def totals_own(r):
        tile, mask = span(r)
        t = nt(mask, window(ownb, tile, whole))
        part[pl.ds(r, 1)] = jnp.concatenate([t[0:1], counts[pl.ds(r, 1), 0:64]], axis=1)

    def gram_a(r):
        tile, mask = span(r)
        right = window(obuf, tile, whole) * mask[0:1]
        ga[slot(r)] = nt(window(obuf, tile, mine), right)

    def gram_b(r):
        tile, mask = span(r)
        right = window(obuf, tile, whole) * mask[0:1]
        return scaled(r, nt(window(y1buf, tile, whole), right), col_y1[r], row_o)

    def two(tile, mask):
        right = jnp.concatenate([window(obuf, tile, mine), window(fbuf, tile, mine)], axis=0)
        return right * mask[0:1]

    def gram_d(r):
        tile, mask = span(r)
        right = window(fbuf, tile, whole) * mask[0:1]
        first = scaled(r, nt(window(y1buf, tile, whole), right), col_y1[r], row_f)
        fk = pl.ds(k1 * 64, 64)
        right = window(obuf, tile, mine) * mask[0:1]
        g = nt(window(fbuf, tile, fk), right)
        g = g * col_f[r, :, 0:64] * row_2[pl.ds(r, 1), 0:64]
        return jnp.concatenate([first, fold(g)], axis=0)

    def gram_c(r):
        tile, mask = span(r)
        g = nt(window(y2buf, tile, whole), two(tile, mask))
        return scaled(r, g, col_y2[r], row_2)

    lo, hi = pl.ds(0, 2), pl.ds(2, 2)
    both_x = pl.ds(0, 2)

    class Sum:
        def __init__(self, g, e1, e2, e3, r1, r2, r3, ss, rs):
            self.g, self.e, self.r = g, (e1, e2, e3), (r1, r2, r3)
            self.ss, self.rs = ss, rs

        def first(self):
            g, r1 = self.g, self.r[0]
            self.c1 = [
                send(g.at[both_x, z2, lo], r1.at[0, 0], self.ss, self.rs, 0, dev_z1),
                send(g.at[both_x, z2, hi], r1.at[1, 0], self.ss, self.rs, 1, dev_z3),
                send(g.at[both_x, z1, lo], r1.at[0, 1], self.ss, self.rs, 2, dev_z1),
                send(g.at[both_x, z3, hi], r1.at[1, 1], self.ss, self.rs, 3, dev_z3),
            ]

        def second(self):
            g, r1, r2 = self.g, self.r[0], self.r[1]
            self.c2 = []
            for p, (js, zz, d) in enumerate(((0, z3, dev_z3), (2, z1, dev_z1))):
                self.c1[p].wait()
                for i in range(2):
                    for j in range(2):
                        g[i, zz, js + j] += r1[p, 0, i, j]
                self.c2.append(send(g.at[both_x, zz, pl.ds(js, 2)], r2.at[p], self.ss, self.rs, 4 + p, d))
            for p in range(2):
                self.c1[2 + p].wait()
                for i in range(2):
                    for j in range(2):
                        g[i, z, 2 * p + j] += r1[p, 1, i, j]

        def third(self):
            g, r2 = self.g, self.r[1]
            for p in range(2):
                self.c2[p].wait()
                for j in range(2):
                    g[1 - xl, z, 2 * p + j] += r2[p, 1 - xl, j]
            self.c3 = send(g.at[1 - xl, z], self.r[2], self.ss, self.rs, 6, dev_x)
            for p in range(2):
                for j in range(2):
                    g[xl, z, 2 * p + j] += r2[p, xl, j]

        def last(self):
            self.c3.wait()

        def total(self, j):
            return self.g[xl, z, j] + self.r[2][j]

    class Direct:
        def __init__(self, body, own, e, r, ss, rs):
            self.body, self.own, self.e, self.r, self.ss, self.rs = body, own, e, r, ss, rs

        def copy(self, q):
            k = q - 1
            return copy(self.e.at[k], self.r.at[k], self.ss.at[k], self.rs.at[k], (tm, (pix + q) % 8))

        def run(self):
            @pl.loop(1, 8)
            def _(q):
                p = (pix + q) % 8
                for j in range(4):
                    self.e[q - 1, j] = encode(self.body(p * 4 + j))
                self.copy(q).start()

            for j in range(4):
                self.own[j] = self.body(pix * 4 + j)

        def wait(self):
            for q in range(1, 8):
                self.copy(q).wait()

        def total(self, j):
            value = self.own[j]
            for q in range(7):
                value = value + decode(self.r[q, j])
            return value

    sum_a = Sum(*set_a)
    class Mixed:
        def __init__(self, body, keepx, keepz, ex, ez, e2x, e2z, rx, rz, r2x, r2z, ss, rs):
            self.body, self.keepx, self.keepz = body, keepx, keepz
            self.ex, self.ez, self.e2x, self.e2z = ex, ez, e2x, e2z
            self.rx, self.rz, self.r2x, self.r2z = rx, rz, r2x, r2z
            self.ss, self.rs = ss, rs

        def go(self, src, dst, k, d):
            return copy(src, dst, self.ss.at[k], self.rs.at[k], d)

        def x_first(self, k):
            return self.go(self.ex.at[k], self.rx.at[k], k, dev_x)

        def z_first(self, q):
            d = (tm, xl * 4 + (z + q) % 4)
            return self.go(self.ez.at[q - 1], self.rz.at[q - 1], 3 + q, d)

        def z_second(self, q):
            d = (tm, xl * 4 + (z + q) % 4)
            return self.go(self.e2x.at[q - 1], self.r2x.at[q - 1], 6 + q, d)

        def x_second(self):
            return self.go(self.e2z, self.r2z, 10, dev_x)

        def run(self):
            @pl.loop(1, 4)
            def _(q):
                for i in range(2):
                    for j in range(2):
                        value = self.body((i * 4 + (z + q) % 4) * 4 + 2 + j)
                        self.ez[q - 1, i, j] = encode(value)
                self.z_first(q).start()

            @pl.loop(0, 4)
            def _(k):
                for j in range(2):
                    self.ex[k, j] = encode(self.body(((1 - xl) * 4 + k) * 4 + j))
                self.x_first(k).start()

            @pl.loop(0, 4)
            def _(k):
                for j in range(2):
                    self.keepx[k, j] = self.body((xl * 4 + k) * 4 + j)

            @pl.loop(0, 2)
            def _(i):
                for j in range(2):
                    self.keepz[i, j] = self.body((i * 4 + z) * 4 + 2 + j)

        def mid(self):
            for k in range(4):
                self.x_first(k).wait()
            for q in range(1, 4):
                k = (z + q) % 4
                for j in range(2):
                    self.e2x[q - 1, j] = encode(self.keepx[k, j] + decode(self.rx[k, j]))
                self.z_second(q).start()
            for q in range(1, 4):
                self.z_first(q).wait()
            for j in range(2):
                self.e2z[j] = encode(self.over_z(1 - xl, j))
            self.x_second().start()

        def over_z(self, i, j):
            value = self.keepz[i, j]
            for q in range(3):
                value = value + decode(self.rz[q, i, j])
            return value

        def wait(self):
            for q in range(1, 4):
                self.z_second(q).wait()
            self.x_second().wait()

        def total(self, j):
            if j < 2:
                value = self.keepx[z, j] + decode(self.rx[z, j])
                for q in range(3):
                    value = value + decode(self.r2x[q, j])
                return value
            return self.over_z(xl, j - 2) + decode(self.r2z[j - 2])

    sum_b, sum_d = Mixed(gram_b, *mixed[0]), Mixed(gram_d, *mixed[1])
    sum_c = Direct(gram_c, *set_c)

    cycles(totals_own)
    pl.semaphore_wait(barrier, len(friends))
    cp = []
    for q in range(1, 8):
        cp.append(send(part, landed.at[q - 1], ps, pr, q - 1, (tm, (pix + q) % 8)))
    pre = pl.ds(0, RELAYED)
    post = pl.ds(RELAYED, obuf.shape[0] - RELAYED)
    dev_prev = at(kx, y + 3, core)
    cp_f = send(ownb, fbuf.at[every, mine], gs, gr, 3, at(1 - kx, y, core))
    cp_y1 = send(ownb, y1buf, gs, gr, 1, dev_prev)
    cp_rel = send(ownb.at[pre], relay, gs, gr, 2, near_core)
    cp_sib = send(ownb, obuf.at[every, mine], gs, gr, 0, dev_sib)
    cp_sib.wait()
    cycles(gram_a)
    sum_a.first()
    total = part[...]
    for q in range(7):
        cp[q].wait()
        total = total + landed[q]
    tt[...] = total
    tcopies = [
        send(tt, tr.at[0], ts, tsr, 0, dev_sib),
        send(tt, tr.at[1], ts, tsr, 1, dev_prev),
        send(tt, tr.at[2], ts, tsr, 2, at(kx, y + 2, flip(core, 1 - ky))),
    ]

    def tcopy(to, slot_core):
        return copy(tt, tr.at[3 + slot_core], ts.at[3 + to], tsr.at[3 + slot_core], at(1 - kx, y, to))

    for c in range(2):
        tcopy(c, core).start()
    sum_a.second()
    cp_rel.wait()
    cp_fr = send(relay, y2buf.at[pre], gs, gr, 7, at(kx, y + 1, flip(core, ((y + 1) % 4) // 2)))
    cp_y1.wait()
    cp_fp = send(y1buf.at[post], y2buf.at[post], gs, gr, 6, at(kx, y + 3, flip(core, ((y + 3) % 4) // 2)))
    for c in tcopies:
        c.wait()
    for c in range(2):
        tcopy(c, core).wait_send()
        tcopy(c, c).wait_recv()

    def pair(first, second):
        return 1.0 / jnp.concatenate([first[:, 0:64], second[:, 0:64]], axis=1)

    def fill(col, table):
        up = (TOP / table.T)[0:64]
        for r in range(CYCLES):
            col[r] = jnp.broadcast_to(up[:, r : r + 1], (64, 128))

    mine_t, sib_t, f0_t, f1_t = tt[...], tr[0], tr[3], tr[4]
    row_o[...] = jnp.where(core == 0, pair(mine_t, sib_t), pair(sib_t, mine_t))
    row_f[...] = pair(f0_t, f1_t)
    row_2[...] = pair(mine_t, jnp.where(core == 0, f0_t, f1_t))
    fill(col_y1, tr[1])

    here = kx * 4 + y
    near = kx * 4 + (y + 1) % 4
    prev = kx * 4 + (y + 3) % 4
    opp = kx * 4 + (y + 2) % 4
    cross = (1 - kx) * 4 + y
    cross_near = (1 - kx) * 4 + (y + 1) % 4
    cross_prev = (1 - kx) * 4 + (y + 3) % 4
    cross_opp = (1 - kx) * 4 + (y + 2) % 4

    def place(j, chip, value):
        value = value * (count(j) * (1.0 / TOP))
        out_ref[j, :, pl.ds(pl.multiple_of(chip * 128, 128), 128)] = value

    def ordered(k, local, remote):
        first = jnp.where(k == 0, local, remote)
        second = jnp.where(k == 0, remote, local)
        return jnp.concatenate([first, second], axis=1)

    def count(j):
        return tt[pl.ds(pix * 4 + j, 1), 64:65]

    def final_a():
        for j in range(4):
            lanes = row_o[pl.ds(pix * 4 + j, 1), :]
            up = (TOP / jnp.broadcast_to(tt[pl.ds(pix * 4 + j, 1), :], (8, 128)).T)[0:64, 0:1]
            place(j, here, sum_a.total(j) * up * lanes)

    def final_b():
        for j in range(4):
            b = sum_b.total(j)
            s1[j] = encode(b)
            bt = b.T
            kept0[j] = jnp.where(core == 0, bt[0:64], bt[64:128])
            s7[j] = encode(fold(jnp.where(core == 0, bt[64:128], bt[0:64])))
        return [
            send(s1, r1, fs, fr, 0, near_core),
            send(s7, r7, fs, fr, 1, dev_sib),
        ]

    def copy4(to, landing):
        return copy(s4.at[to], r4.at[landing], fs.at[2 + to], fr.at[2 + landing], at(1 - kx, y, to))

    def final_d():
        for j in range(4):
            g = sum_d.total(j)
            s2[j] = encode(g[0:64])
            dt = g[0:64].T
            s4[0, j] = encode(fold(dt[0:64]))
            s4[1, j] = encode(fold(dt[64:128]))
            s6[j] = encode(g[64:96])
            kept1[j] = unfold(g[64:96]).T
        for c in range(2):
            copy4(c, core).start()
        return [
            send(s2, r2, fs, fr, 4, near_core),
            send(s6, r6, fs, fr, 5, at(1 - kx, y, k1)),
        ]

    def final_c():
        for j in range(4):
            e = sum_c.total(j)
            s3[j] = encode(e)
            et = e.T
            kept2[j] = et[0:64]
            s5[j] = encode(fold(et[64:128]))
        return [
            send(s3, r3, fs, fr, 6, at(kx, y + 2, k2)),
            send(s5, r5, fs, fr, 7, at(1 - kx, y, core)),
        ]

    cp_f.wait()
    fw_f = send(fbuf.at[every, mine], fbuf.at[every, mine], gs, gr, 4, dev_sib)
    sum_b.run()
    fill(col_f, jnp.where(k1 == 0, f0_t, f1_t))
    fw_f.wait()
    sum_d.run()
    sum_a.third()
    sum_b.mid()
    fill(col_y2, tr[2])
    cp_fp.wait()
    cp_fr.wait()
    sum_c.run()
    sum_d.mid()
    sum_a.last()
    final_a()
    sum_b.wait()
    out_b = final_b()
    sum_d.wait()
    out_d = final_d()
    sum_c.wait()
    out_c = final_c()
    for c in out_b:
        c.wait()
    for j in range(4):
        place(j, near, ordered(core, kept0[j], unfold(decode(r7[j]))))
        place(j, prev, decode(r1[j]))

    for c in range(2):
        copy4(c, core).wait_send()
        copy4(c, c).wait_recv()
    for c in out_d:
        c.wait()
    for j in range(4):
        place(j, cross_near, jnp.concatenate([unfold(decode(r4[0, j])), unfold(decode(r4[1, j]))], axis=1))
        place(j, cross_prev, decode(r2[j]))
        place(j, cross, ordered(k1, kept1[j], unfold(decode(r6[j]))))
    for c in out_c:
        c.wait()
    for j in range(4):
        far = decode(r3[j])
        place(j, opp, ordered(k2, kept2[j], far[:, 0:64]))
        place(j, cross_opp, ordered(k2, unfold(decode(r5[j])), far[:, 64:128]))


def per_device(intensity, labels):
    tile_lab = labels.reshape(-1, 128)[:, 0]
    cycles = jnp.arange(CYCLES, dtype=jnp.int32)
    first = jnp.sum((tile_lab[None, :] < cycles[:, None]).astype(jnp.int32), axis=1)
    count = jnp.sum((tile_lab[None, :] == cycles[:, None]).astype(jnp.int32), axis=1)
    places = jnp.minimum(first, tile_lab.shape[0] - CAP)
    low = (first - places) * 128
    high = low + count * 128
    lane = jnp.arange(CAP * 128, dtype=jnp.int32)[None, :]
    masks = ((lane >= low[:, None]) & (lane < high[:, None])).astype(F32)
    counts = jnp.broadcast_to((count * 128).astype(F32)[:, None], (CYCLES, 128))
    pix_dev = intensity.shape[1]
    dma = pltpu.SemaphoreType.DMA

    halves = [
        pltpu.VMEM((2, 2, 2, 2, ROWS_A, 128), F32),
        pltpu.VMEM((2, 2, 2, ROWS_A, 128), F32),
        pltpu.VMEM((4, ROWS_A, 128), F32),
    ]

    def two_ways(rows):
        def codes(*lead):
            return pltpu.VMEM((*lead, rows, 128), CODE)

        moved = [codes(4, 2), codes(3, 2, 2), codes(3, 2), codes(2)]
        kept = [pltpu.VMEM((4, 2, rows, 128), F32), pltpu.VMEM((2, 2, rows, 128), F32)]
        return [*kept, *moved, *moved, dma((11,)), dma((11,))]

    def direct(rows):
        slabs = pltpu.VMEM((7, 4, rows, 128), CODE)
        return [pltpu.VMEM((4, rows, 128), F32), slabs, slabs, dma((7,)), dma((7,))]

    big = pltpu.VMEM((4, 64, 128), CODE)
    small = pltpu.VMEM((4, 32, 128), CODE)
    messages = [big, big, big, pltpu.VMEM((2, 4, 32, 128), CODE), small, small, small]
    kept = pltpu.VMEM((4, 64, 64), F32)
    tiles = pix_dev // 128
    return pl.pallas_call(
        kernel,
        out_shape=jax.ShapeDtypeStruct((4, 64, 1024), F32),
        in_specs=[
            pl.BlockSpec(memory_space=pltpu.SMEM),
            pl.BlockSpec(memory_space=pltpu.VMEM),
            pl.BlockSpec(memory_space=pltpu.VMEM),
            pl.BlockSpec(memory_space=pltpu.HBM),
        ],
        out_specs=pl.BlockSpec(memory_space=pltpu.VMEM),
        scratch_shapes=[
            pltpu.VMEM((FRAMES_DEV, pix_dev), BF16),
            pltpu.VMEM((tiles, FRAMES_DEV, 128), BF16),
            pltpu.VMEM((tiles, 2 * FRAMES_DEV, 128), BF16),
            pltpu.VMEM((tiles, 2 * FRAMES_DEV, 128), BF16),
            pltpu.VMEM((tiles, FRAMES_DEV, 128), BF16),
            pltpu.VMEM((tiles, FRAMES_DEV, 128), BF16),
            pltpu.VMEM((RELAYED, FRAMES_DEV, 128), BF16),
            pltpu.VMEM((CYCLES, 128), F32),
            pltpu.VMEM((7, CYCLES, 128), F32),
            pltpu.VMEM((CYCLES, 128), F32),
            pltpu.VMEM((5, CYCLES, 128), F32),
            *[pltpu.VMEM((CYCLES, FRAMES_DEV, 128), F32)] * 3,
            *[pltpu.VMEM((CYCLES, 128), F32)] * 3,
            pltpu.VMEM((2, 4, 4, ROWS_A, 128), F32),
            *halves,
            *halves,
            dma((7,)),
            dma((7,)),
            *[ref for rows in MIXED for ref in two_ways(rows)],
            *direct(DIRECT),
            *messages,
            *messages,
            kept,
            kept,
            kept,
            dma,
            dma((8,)),
            dma((8,)),
            dma((7,)),
            dma((7,)),
            dma((5,)),
            dma((5,)),
            dma((8,)),
            dma((8,)),
        ],
        compiler_params=pltpu.CompilerParams(
            collective_id=0, has_side_effects=True, vmem_limit_bytes=48 * 2**20
        ),
    )(places, masks, counts, intensity)


def solution(mesh):
    placed = (P("tm", "pix"), P("pix"))
    return jax.shard_map(
        per_device, mesh=mesh, in_specs=placed, out_specs=P("pix", "tm", None), check_vma=False
    )
```

```python
import jax
import jax.numpy as jnp
from jax import lax
from jax.experimental import pallas as pl
from jax.experimental.pallas import tpu as pltpu
from jax.sharding import PartitionSpec as P

CYCLES = 32
CAP = 4
MESH = pl.DeviceIdType.MESH
F32 = jnp.float32
BF16 = jnp.bfloat16
FRAMES_DEV = 64
TOP = 32768.0
STEPS = 2048.0
CODE = jnp.int16
ROWS_A = 64
MIXED = (64, 96)
DIRECT = 64
RELAYED = 36


def nt(left, right):
    return lax.dot_general(left, right, (((1,), (1,)), ((), ())), preferred_element_type=F32)


def encode(value):
    level = jnp.log2(jnp.maximum(value, 1.0 / 65536.0)) * STEPS
    return jnp.round(level).astype(jnp.int32).astype(CODE)


def decode(code):
    return jnp.exp2(code.astype(jnp.int32).astype(F32) * (1.0 / STEPS))


def fold(block):
    return jnp.concatenate([block[0:32], block[32:64]], axis=1)


def unfold(block):
    return jnp.concatenate([block[:, 0:64], block[:, 64:128]], axis=0)


def kernel(places, masks, counts, x_ref, out_ref, *refs):
    refs = list(refs)

    def take(n):
        got = refs[:n]
        del refs[:n]
        return got

    xv, ownb, obuf, fbuf, y1buf, y2buf, relay = take(7)
    part, landed, tt, tr = take(4)
    col_y1, col_y2, col_f = take(3)
    row_o, row_f, row_2 = take(3)
    set_a = take(9)
    mixed = [take(12) for _ in MIXED]
    set_c = take(5)
    s1, s2, s3, s4, s5, s6, s7 = take(7)
    r1, r2, r3, r4, r5, r6, r7 = take(7)
    kept0, kept1, kept2 = take(3)
    own_sem, gs, gr, ps, pr, ts, tsr, fs, fr = take(9)

    tm, pix = lax.axis_index("tm"), lax.axis_index("pix")
    core = tm % 2
    y = (tm // 2) % 4
    kx = tm // 8
    ky = y // 2
    z = pix % 4
    xl = pix // 4
    sib = 1 - core

    def at(k, yy, c):
        return ((k * 4 + yy % 4) * 2 + c, pix)

    def flip(a, b):
        return (a + b) % 2

    k2 = flip(core, ky)
    k1 = flip(core, kx)
    z1 = z + 1 - 2 * (z % 2)
    z3 = 3 - z
    z2 = (z + 2) % 4
    dev_sib = at(kx, y, sib)
    dev_z1 = (tm, xl * 4 + z1)
    dev_z3 = (tm, xl * 4 + z3)
    dev_x = (tm, (1 - xl) * 4 + z)
    near_core = at(kx, y + 1, core)

    own = pltpu.make_async_copy(x_ref, xv, own_sem)
    own.start()
    barrier = pltpu.get_barrier_semaphore()
    friends = [dev_sib] + [(tm, (pix + q) % 8) for q in range(1, 8)]
    for c in range(2):
        friends += [at(kx, y + 1, c), at(kx, y + 3, c), at(kx, y + 2, c), at(1 - kx, y, c)]
    for d in friends:
        pl.semaphore_signal(barrier, inc=1, device_id=d, device_id_type=MESH)
    mine = pl.ds(core * 64, 64)
    own.wait()
    for t in range(x_ref.shape[1] // 128):
        block = xv[:, t * 128 : t * 128 + 128]
        ownb[t] = block
        obuf[t, mine] = block

    def copy(src, dst, ss, rs, d):
        return pltpu.make_async_remote_copy(
            src_ref=src, dst_ref=dst, send_sem=ss, recv_sem=rs, device_id=d, device_id_type=MESH
        )

    def send(src, dst, ss, rs, k, d):
        r = copy(src, dst, ss.at[k], rs.at[k], d)
        r.start()
        return r

    every = pl.ds(0, obuf.shape[0])
    def span(r):
        tile = places[r]
        mask = jnp.broadcast_to(masks[pl.ds(r, 1), :], (8, CAP * 128)).astype(BF16)
        return tile, mask

    def window(ref, tile, rows):
        return jnp.concatenate([ref[tile + k, rows] for k in range(CAP)], axis=1)

    def slot(r):
        return r // 16, (r // 4) % 4, r % 4

    def cycles(body):
        @pl.loop(0, CYCLES, unroll=4)
        def _(r):
            body(r)

    ga = set_a[0]
    whole = slice(None)

    def scaled(r, g, col, rows):
        return g * col * rows[pl.ds(r, 1), :]

    def totals_own(r):
        tile, mask = span(r)
        t = nt(mask, window(ownb, tile, whole))
        part[pl.ds(r, 1)] = jnp.concatenate([t[0:1], counts[pl.ds(r, 1), 0:64]], axis=1)

    def gram_a(r):
        tile, mask = span(r)
        right = window(obuf, tile, whole) * mask[0:1]
        ga[slot(r)] = nt(window(obuf, tile, mine), right)

    def gram_b(r):
        tile, mask = span(r)
        right = window(obuf, tile, whole) * mask[0:1]
        return scaled(r, nt(window(y1buf, tile, whole), right), col_y1[r], row_o)

    def two(tile, mask):
        right = jnp.concatenate([window(obuf, tile, mine), window(fbuf, tile, mine)], axis=0)
        return right * mask[0:1]

    def gram_d(r):
        tile, mask = span(r)
        right = window(fbuf, tile, whole) * mask[0:1]
        first = scaled(r, nt(window(y1buf, tile, whole), right), col_y1[r], row_f)
        fk = pl.ds(k1 * 64, 64)
        right = window(obuf, tile, mine) * mask[0:1]
        g = nt(window(fbuf, tile, fk), right)
        g = g * col_f[r, :, 0:64] * row_2[pl.ds(r, 1), 0:64]
        return jnp.concatenate([first, fold(g)], axis=0)

    def gram_c(r):
        tile, mask = span(r)
        g = nt(window(y2buf, tile, whole), two(tile, mask))
        return scaled(r, g, col_y2[r], row_2)

    lo, hi = pl.ds(0, 2), pl.ds(2, 2)
    both_x = pl.ds(0, 2)

    class Sum:
        def __init__(self, g, e1, e2, e3, r1, r2, r3, ss, rs):
            self.g, self.e, self.r = g, (e1, e2, e3), (r1, r2, r3)
            self.ss, self.rs = ss, rs

        def first(self):
            g, r1 = self.g, self.r[0]
            self.c1 = [
                send(g.at[both_x, z2, lo], r1.at[0, 0], self.ss, self.rs, 0, dev_z1),
                send(g.at[both_x, z2, hi], r1.at[1, 0], self.ss, self.rs, 1, dev_z3),
                send(g.at[both_x, z1, lo], r1.at[0, 1], self.ss, self.rs, 2, dev_z1),
                send(g.at[both_x, z3, hi], r1.at[1, 1], self.ss, self.rs, 3, dev_z3),
            ]

        def second(self):
            g, r1, r2 = self.g, self.r[0], self.r[1]
            self.c2 = []
            for p, (js, zz, d) in enumerate(((0, z3, dev_z3), (2, z1, dev_z1))):
                self.c1[p].wait()
                for i in range(2):
                    for j in range(2):
                        g[i, zz, js + j] += r1[p, 0, i, j]
                self.c2.append(send(g.at[both_x, zz, pl.ds(js, 2)], r2.at[p], self.ss, self.rs, 4 + p, d))
            for p in range(2):
                self.c1[2 + p].wait()
                for i in range(2):
                    for j in range(2):
                        g[i, z, 2 * p + j] += r1[p, 1, i, j]

        def third(self):
            g, r2 = self.g, self.r[1]
            for p in range(2):
                self.c2[p].wait()
                for j in range(2):
                    g[1 - xl, z, 2 * p + j] += r2[p, 1 - xl, j]
            self.c3 = send(g.at[1 - xl, z], self.r[2], self.ss, self.rs, 6, dev_x)
            for p in range(2):
                for j in range(2):
                    g[xl, z, 2 * p + j] += r2[p, xl, j]

        def last(self):
            self.c3.wait()

        def total(self, j):
            return self.g[xl, z, j] + self.r[2][j]

    class Direct:
        def __init__(self, body, own, e, r, ss, rs):
            self.body, self.own, self.e, self.r, self.ss, self.rs = body, own, e, r, ss, rs

        def copy(self, q):
            k = q - 1
            return copy(self.e.at[k], self.r.at[k], self.ss.at[k], self.rs.at[k], (tm, (pix + q) % 8))

        def run(self):
            @pl.loop(1, 8)
            def _(q):
                p = (pix + q) % 8
                for j in range(4):
                    self.e[q - 1, j] = encode(self.body(p * 4 + j))
                self.copy(q).start()

            for j in range(4):
                self.own[j] = self.body(pix * 4 + j)

        def wait(self):
            for q in range(1, 8):
                self.copy(q).wait()

        def total(self, j):
            value = self.own[j]
            for q in range(7):
                value = value + decode(self.r[q, j])
            return value

    sum_a = Sum(*set_a)
    class Mixed:
        def __init__(self, body, keepx, keepz, ex, ez, e2x, e2z, rx, rz, r2x, r2z, ss, rs):
            self.body, self.keepx, self.keepz = body, keepx, keepz
            self.ex, self.ez, self.e2x, self.e2z = ex, ez, e2x, e2z
            self.rx, self.rz, self.r2x, self.r2z = rx, rz, r2x, r2z
            self.ss, self.rs = ss, rs

        def go(self, src, dst, k, d):
            return copy(src, dst, self.ss.at[k], self.rs.at[k], d)

        def x_first(self, k):
            return self.go(self.ex.at[k], self.rx.at[k], k, dev_x)

        def z_first(self, q):
            d = (tm, xl * 4 + (z + q) % 4)
            return self.go(self.ez.at[q - 1], self.rz.at[q - 1], 3 + q, d)

        def z_second(self, q):
            d = (tm, xl * 4 + (z + q) % 4)
            return self.go(self.e2x.at[q - 1], self.r2x.at[q - 1], 6 + q, d)

        def x_second(self):
            return self.go(self.e2z, self.r2z, 10, dev_x)

        def run(self):
            @pl.loop(1, 4)
            def _(q):
                for i in range(2):
                    for j in range(2):
                        value = self.body((i * 4 + (z + q) % 4) * 4 + 2 + j)
                        self.ez[q - 1, i, j] = encode(value)
                self.z_first(q).start()

            @pl.loop(0, 4)
            def _(k):
                for j in range(2):
                    self.ex[k, j] = encode(self.body(((1 - xl) * 4 + k) * 4 + j))
                self.x_first(k).start()

            @pl.loop(0, 4)
            def _(k):
                for j in range(2):
                    self.keepx[k, j] = self.body((xl * 4 + k) * 4 + j)

            @pl.loop(0, 2)
            def _(i):
                for j in range(2):
                    self.keepz[i, j] = self.body((i * 4 + z) * 4 + 2 + j)

        def mid(self):
            for k in range(4):
                self.x_first(k).wait()
            for q in range(1, 4):
                k = (z + q) % 4
                for j in range(2):
                    self.e2x[q - 1, j] = encode(self.keepx[k, j] + decode(self.rx[k, j]))
                self.z_second(q).start()
            for q in range(1, 4):
                self.z_first(q).wait()
            for j in range(2):
                self.e2z[j] = encode(self.over_z(1 - xl, j))
            self.x_second().start()

        def over_z(self, i, j):
            value = self.keepz[i, j]
            for q in range(3):
                value = value + decode(self.rz[q, i, j])
            return value

        def wait(self):
            for q in range(1, 4):
                self.z_second(q).wait()
            self.x_second().wait()

        def total(self, j):
            if j < 2:
                value = self.keepx[z, j] + decode(self.rx[z, j])
                for q in range(3):
                    value = value + decode(self.r2x[q, j])
                return value
            return self.over_z(xl, j - 2) + decode(self.r2z[j - 2])

    sum_b, sum_d = Mixed(gram_b, *mixed[0]), Mixed(gram_d, *mixed[1])
    sum_c = Direct(gram_c, *set_c)

    cycles(totals_own)
    pl.semaphore_wait(barrier, len(friends))
    cp = []
    for q in range(1, 8):
        cp.append(send(part, landed.at[q - 1], ps, pr, q - 1, (tm, (pix + q) % 8)))
    pre = pl.ds(0, RELAYED)
    post = pl.ds(RELAYED, obuf.shape[0] - RELAYED)
    dev_prev = at(kx, y + 3, core)
    cp_f = send(ownb, fbuf.at[every, mine], gs, gr, 3, at(1 - kx, y, core))
    cp_y1 = send(ownb, y1buf, gs, gr, 1, dev_prev)
    cp_rel = send(ownb.at[pre], relay, gs, gr, 2, near_core)
    cp_sib = send(ownb, obuf.at[every, mine], gs, gr, 0, dev_sib)
    cp_sib.wait()
    cycles(gram_a)
    sum_a.first()
    total = part[...]
    for q in range(7):
        cp[q].wait()
        total = total + landed[q]
    tt[...] = total
    tcopies = [
        send(tt, tr.at[0], ts, tsr, 0, dev_sib),
        send(tt, tr.at[1], ts, tsr, 1, dev_prev),
        send(tt, tr.at[2], ts, tsr, 2, at(kx, y + 2, flip(core, 1 - ky))),
    ]

    def tcopy(to, slot_core):
        return copy(tt, tr.at[3 + slot_core], ts.at[3 + to], tsr.at[3 + slot_core], at(1 - kx, y, to))

    for c in range(2):
        tcopy(c, core).start()
    sum_a.second()
    cp_rel.wait()
    cp_fr = send(relay, y2buf.at[pre], gs, gr, 7, at(kx, y + 1, flip(core, ((y + 1) % 4) // 2)))
    cp_y1.wait()
    cp_fp = send(y1buf.at[post], y2buf.at[post], gs, gr, 6, at(kx, y + 3, flip(core, ((y + 3) % 4) // 2)))
    for c in tcopies:
        c.wait()
    for c in range(2):
        tcopy(c, core).wait_send()
        tcopy(c, c).wait_recv()

    def pair(first, second):
        return 1.0 / jnp.concatenate([first[:, 0:64], second[:, 0:64]], axis=1)

    def fill(col, table):
        up = (TOP / table.T)[0:64]
        for r in range(CYCLES):
            col[r] = jnp.broadcast_to(up[:, r : r + 1], (64, 128))

    mine_t, sib_t, f0_t, f1_t = tt[...], tr[0], tr[3], tr[4]
    row_o[...] = jnp.where(core == 0, pair(mine_t, sib_t), pair(sib_t, mine_t))
    row_f[...] = pair(f0_t, f1_t)
    row_2[...] = pair(mine_t, jnp.where(core == 0, f0_t, f1_t))
    fill(col_y1, tr[1])

    here = kx * 4 + y
    near = kx * 4 + (y + 1) % 4
    prev = kx * 4 + (y + 3) % 4
    opp = kx * 4 + (y + 2) % 4
    cross = (1 - kx) * 4 + y
    cross_near = (1 - kx) * 4 + (y + 1) % 4
    cross_prev = (1 - kx) * 4 + (y + 3) % 4
    cross_opp = (1 - kx) * 4 + (y + 2) % 4

    def place(j, chip, value):
        value = value * (count(j) * (1.0 / TOP))
        out_ref[j, :, pl.ds(pl.multiple_of(chip * 128, 128), 128)] = value

    def ordered(k, local, remote):
        first = jnp.where(k == 0, local, remote)
        second = jnp.where(k == 0, remote, local)
        return jnp.concatenate([first, second], axis=1)

    def count(j):
        return tt[pl.ds(pix * 4 + j, 1), 64:65]

    def final_a():
        for j in range(4):
            lanes = row_o[pl.ds(pix * 4 + j, 1), :]
            up = (TOP / jnp.broadcast_to(tt[pl.ds(pix * 4 + j, 1), :], (8, 128)).T)[0:64, 0:1]
            place(j, here, sum_a.total(j) * up * lanes)

    def final_b():
        for j in range(4):
            b = sum_b.total(j)
            s1[j] = encode(b)
            bt = b.T
            kept0[j] = jnp.where(core == 0, bt[0:64], bt[64:128])
            s7[j] = encode(fold(jnp.where(core == 0, bt[64:128], bt[0:64])))
        return [
            send(s1, r1, fs, fr, 0, near_core),
            send(s7, r7, fs, fr, 1, dev_sib),
        ]

    def copy4(to, landing):
        return copy(s4.at[to], r4.at[landing], fs.at[2 + to], fr.at[2 + landing], at(1 - kx, y, to))

    def final_d():
        for j in range(4):
            g = sum_d.total(j)
            s2[j] = encode(g[0:64])
            dt = g[0:64].T
            s4[0, j] = encode(fold(dt[0:64]))
            s4[1, j] = encode(fold(dt[64:128]))
            s6[j] = encode(g[64:96])
            kept1[j] = unfold(g[64:96]).T
        for c in range(2):
            copy4(c, core).start()
        return [
            send(s2, r2, fs, fr, 4, near_core),
            send(s6, r6, fs, fr, 5, at(1 - kx, y, k1)),
        ]

    def final_c():
        for j in range(4):
            e = sum_c.total(j)
            s3[j] = encode(e)
            et = e.T
            kept2[j] = et[0:64]
            s5[j] = encode(fold(et[64:128]))
        return [
            send(s3, r3, fs, fr, 6, at(kx, y + 2, k2)),
            send(s5, r5, fs, fr, 7, at(1 - kx, y, core)),
        ]

    cp_f.wait()
    fw_f = send(fbuf.at[every, mine], fbuf.at[every, mine], gs, gr, 4, dev_sib)
    sum_b.run()
    fill(col_f, jnp.where(k1 == 0, f0_t, f1_t))
    fw_f.wait()
    sum_d.run()
    sum_a.third()
    sum_b.mid()
    fill(col_y2, tr[2])
    cp_fp.wait()
    cp_fr.wait()
    sum_c.run()
    sum_d.mid()
    sum_a.last()
    final_a()
    sum_b.wait()
    out_b = final_b()
    sum_d.wait()
    out_d = final_d()
    sum_c.wait()
    out_c = final_c()
    for c in out_b:
        c.wait()
    for j in range(4):
        place(j, near, ordered(core, kept0[j], unfold(decode(r7[j]))))
        place(j, prev, decode(r1[j]))

    for c in range(2):
        copy4(c, core).wait_send()
        copy4(c, c).wait_recv()
    for c in out_d:
        c.wait()
    for j in range(4):
        place(j, cross_near, jnp.concatenate([unfold(decode(r4[0, j])), unfold(decode(r4[1, j]))], axis=1))
        place(j, cross_prev, decode(r2[j]))
        place(j, cross, ordered(k1, kept1[j], unfold(decode(r6[j]))))
    for c in out_c:
        c.wait()
    for j in range(4):
        far = decode(r3[j])
        place(j, opp, ordered(k2, kept2[j], far[:, 0:64]))
        place(j, cross_opp, ordered(k2, unfold(decode(r5[j])), far[:, 64:128]))


def per_device(intensity, labels):
    tile_lab = labels.reshape(-1, 128)[:, 0]
    cycles = jnp.arange(CYCLES, dtype=jnp.int32)
    first = jnp.sum((tile_lab[None, :] < cycles[:, None]).astype(jnp.int32), axis=1)
    count = jnp.sum((tile_lab[None, :] == cycles[:, None]).astype(jnp.int32), axis=1)
    places = jnp.minimum(first, tile_lab.shape[0] - CAP)
    low = (first - places) * 128
    high = low + count * 128
    lane = jnp.arange(CAP * 128, dtype=jnp.int32)[None, :]
    masks = ((lane >= low[:, None]) & (lane < high[:, None])).astype(F32)
    counts = jnp.broadcast_to((count * 128).astype(F32)[:, None], (CYCLES, 128))
    pix_dev = intensity.shape[1]
    dma = pltpu.SemaphoreType.DMA

    halves = [
        pltpu.VMEM((2, 2, 2, 2, ROWS_A, 128), F32),
        pltpu.VMEM((2, 2, 2, ROWS_A, 128), F32),
        pltpu.VMEM((4, ROWS_A, 128), F32),
    ]

    def two_ways(rows):
        def codes(*lead):
            return pltpu.VMEM((*lead, rows, 128), CODE)

        moved = [codes(4, 2), codes(3, 2, 2), codes(3, 2), codes(2)]
        kept = [pltpu.VMEM((4, 2, rows, 128), F32), pltpu.VMEM((2, 2, rows, 128), F32)]
        return [*kept, *moved, *moved, dma((11,)), dma((11,))]

    def direct(rows):
        slabs = pltpu.VMEM((7, 4, rows, 128), CODE)
        return [pltpu.VMEM((4, rows, 128), F32), slabs, slabs, dma((7,)), dma((7,))]

    big = pltpu.VMEM((4, 64, 128), CODE)
    small = pltpu.VMEM((4, 32, 128), CODE)
    messages = [big, big, big, pltpu.VMEM((2, 4, 32, 128), CODE), small, small, small]
    kept = pltpu.VMEM((4, 64, 64), F32)
    tiles = pix_dev // 128
    return pl.pallas_call(
        kernel,
        out_shape=jax.ShapeDtypeStruct((4, 64, 1024), F32),
        in_specs=[
            pl.BlockSpec(memory_space=pltpu.SMEM),
            pl.BlockSpec(memory_space=pltpu.VMEM),
            pl.BlockSpec(memory_space=pltpu.VMEM),
            pl.BlockSpec(memory_space=pltpu.HBM),
        ],
        out_specs=pl.BlockSpec(memory_space=pltpu.VMEM),
        scratch_shapes=[
            pltpu.VMEM((FRAMES_DEV, pix_dev), BF16),
            pltpu.VMEM((tiles, FRAMES_DEV, 128), BF16),
            pltpu.VMEM((tiles, 2 * FRAMES_DEV, 128), BF16),
            pltpu.VMEM((tiles, 2 * FRAMES_DEV, 128), BF16),
            pltpu.VMEM((tiles, FRAMES_DEV, 128), BF16),
            pltpu.VMEM((tiles, FRAMES_DEV, 128), BF16),
            pltpu.VMEM((RELAYED, FRAMES_DEV, 128), BF16),
            pltpu.VMEM((CYCLES, 128), F32),
            pltpu.VMEM((7, CYCLES, 128), F32),
            pltpu.VMEM((CYCLES, 128), F32),
            pltpu.VMEM((5, CYCLES, 128), F32),
            *[pltpu.VMEM((CYCLES, FRAMES_DEV, 128), F32)] * 3,
            *[pltpu.VMEM((CYCLES, 128), F32)] * 3,
            pltpu.VMEM((2, 4, 4, ROWS_A, 128), F32),
            *halves,
            *halves,
            dma((7,)),
            dma((7,)),
            *[ref for rows in MIXED for ref in two_ways(rows)],
            *direct(DIRECT),
            *messages,
            *messages,
            kept,
            kept,
            kept,
            dma,
            dma((8,)),
            dma((8,)),
            dma((7,)),
            dma((7,)),
            dma((5,)),
            dma((5,)),
            dma((8,)),
            dma((8,)),
        ],
        compiler_params=pltpu.CompilerParams(
            collective_id=0, has_side_effects=True, vmem_limit_bytes=48 * 2**20
        ),
    )(places, masks, counts, intensity)


def solution(mesh):
    placed = (P("tm", "pix"), P("pix"))
    return jax.shard_map(
        per_device, mesh=mesh, in_specs=placed, out_specs=P("pix", "tm", None), check_vma=False
    )
```
